32 devices in a mesh: mode: 4 (over y, x), mer: 8 (over z, core).
Axes of the slice: x: 2, y: 2, z: 4, core: 2. Of those that a mesh axis runs over, the one named last changes fastest.
Arguments:
- field: float32 [32, 6, 4096], P('mode', None, 'mer'), may hold values from -6 to 6
- velocity: bfloat16 [3, 64, 4096], P(None, None, ('mer', 'mode')), may hold values from -4 to 4
- stiffness: float32 [64, 64], replicated, may hold values from -0.75 to 0.75
- curl_matrix: float32 [64, 64], replicated, may hold values from -0.75 to 0.75
- mass: float32 [4096], P('mer'), may hold values from 0.5 to 2
- connect: int32 [128, 64], P('mer'), may hold values from 0 to 767
- wall_index: int32 [512], P('mer'), may hold values from 0 to 511, as said below
- dtn: bfloat16 [32, 512, 512], P('mode', 'mer'), as said below
Outputs:
- advanced: float32 [32, 6, 4096], P('mode', None, 'mer')
- wall_flux: float32 [2, 32, 2, 512], P(None, 'mode', None, 'mer')
The draws below stay inside these ranges and needn't reach their ends.
Inputs may be any that keep to these rules, and one draw needn't show every extreme that they name: `wall_index`: within each block of 64 consecutive entries the numbers are distinct. `dtn`: each mode's matrix is symmetric.
All inputs are finite; a program needn't handle non-finite values.
Results may differ from the reference program's by a relative error of at most 0.005.
Values may be sent and summed in bfloat16 or wider, within the bound.
A program may use at most 64 MiB of HBM per device.

```python
import math
import jax
import jax.numpy as jnp
from jax import lax

MODES = 32
NPHI = 64
NODES_DEV = 512
NODES = 4096
GHOST = 256
ELEM_DEV = 16
ELEMS = 128
NP = 64
WALL_DEV = 64
WALL = 512


def draw_wall_index(key, part):
    blocks = WALL // WALL_DEV
    scores = jax.random.randint(key, (blocks, NODES_DEV), 0, 1 << 20)
    scores = scores * NODES_DEV + jnp.arange(NODES_DEV, dtype=jnp.int32)[None, :]
    order = jnp.argsort(scores, axis=1, stable=True)
    return order[:, :WALL_DEV].reshape(WALL).astype(jnp.int32)


def draw_dtn(key, part):
    base = jax.random.normal(key, (MODES, WALL, WALL), jnp.float32) * WALL ** (-0.5)
    sym = 0.5 * (base + jnp.swapaxes(base, 1, 2))
    sym = sym + jnp.eye(WALL, dtype=jnp.float32)[None]
    return sym.astype(jnp.bfloat16)


def place_ends(values, stream_key, smallest, high):
    longest = values.shape.index(max(values.shape))
    spots = []
    for shift in (0, 1):
        where = [jax.random.randint(jax.random.fold_in(stream_key, axis), (), 0, length) for axis, length in enumerate(values.shape)]
        where[longest] = (where[longest] + shift) % values.shape[longest]
        spots.append(tuple(where))
    return values.at[spots[0]].set(smallest).at[spots[1]].set(high)


def steps_of(key, extent, cuts, low, high):
    gain, own = 1.0, jax.random.fold_in(key, 6)
    for position, shards_of in cuts:
        draws = jnp.exp(jax.random.uniform(jax.random.fold_in(own, position), (shards_of,), jnp.float32, low / len(cuts), high / len(cuts)))
        gain = gain * jnp.repeat(draws, extent[position] // shards_of).reshape([-1 if axis == position else 1 for axis in range(len(extent))])
    return gain


def scatter_about(own_key, dims, deviation, limit, cuts=(), held_as=jnp.bfloat16):
    entries = deviation * jax.random.normal(own_key, dims, jnp.float32)
    if cuts:
        entries = entries * steps_of(own_key, dims, cuts, -0.22, 0.18)
    return jnp.clip(entries, -limit, limit).astype(held_as)


def setup_inputs(seed: int = 0) -> dict:
    key_of = jax.random.split(jax.random.key(seed), 9)
    return {
        "field": scatter_about(key_of[0], (MODES, 6, NODES), 1.0, 6.0, ((0, 4), (2, 8)), jnp.float32),
        "velocity": scatter_about(key_of[1], (3, NPHI, NODES), 0.5, 4.0, ((2, 32),)),
        "stiffness": scatter_about(key_of[2], (NP, NP), NP ** -0.5, 0.75, (), jnp.float32),
        "curl_matrix": scatter_about(key_of[3], (NP, NP), NP ** -0.5, 0.75, (), jnp.float32),
        "mass": jnp.clip(jnp.exp(math.log(2.0) - 1.3862944 * jax.random.uniform(key_of[4], (NODES,), jnp.float32) ** steps_of(key_of[4], (NODES,), ((0, 8),), -0.2, 0.2)), 0.5, 2.0),
        "connect": place_ends(jax.random.randint(key_of[5], (ELEMS, NP), 0, NODES_DEV + GHOST), jax.random.fold_in(key_of[5], 1), 0, (NODES_DEV + GHOST) - 1).astype(jnp.int32),
        "wall_index": draw_wall_index(jax.random.fold_in(key_of[8], 71), 0),
        "dtn": draw_dtn(jax.random.fold_in(key_of[8], 71), 0),
    }


HI = lax.Precision.HIGHEST


def tables(modes, nphi):
    m = jnp.arange(modes, dtype=jnp.float32)
    k = jnp.arange(nphi, dtype=jnp.float32)
    angle = 2.0 * jnp.pi * m[:, None] * k[None, :] / nphi
    forward = jnp.stack([jnp.cos(angle), -jnp.sin(angle)], 1)
    return forward, forward / nphi


def induced(field, velocity):
    modes = field.shape[0]
    nphi = velocity.shape[1]
    forward, inverse = tables(modes, nphi)
    phys = jnp.einsum('mpcn,mpk->ckn', field.reshape(modes, 2, 3, -1), forward, precision=HI)
    vel = velocity.astype(jnp.float32)
    cross = jnp.stack([vel[1] * phys[2] - vel[2] * phys[1], vel[2] * phys[0] - vel[0] * phys[2], vel[0] * phys[1] - vel[1] * phys[0]])
    back = jnp.einsum('ckn,mpk->mpcn', cross, inverse, precision=HI)
    return back.reshape(modes, 6, -1)


def rate(field, velocity, stiffness, curl_matrix, mass, connect, wall_index, dtn):
    emf = induced(field, velocity)
    block = jnp.arange(ELEMS, dtype=jnp.int32) // ELEM_DEV
    glob = block[:, None] * NODES_DEV + connect
    valid = (glob < NODES).T
    where_node = jnp.where(glob < NODES, glob, 0).T

    def one_mode(pair):
        fmode, emode = pair
        values = jnp.where(valid, fmode[:, where_node], 0.0)
        evals = jnp.where(valid, emode[:, where_node], 0.0).reshape(2, 3, NP, -1)
        evals = jnp.roll(evals, 1, axis=1).reshape(6, NP, -1)
        local = -1.0 * jnp.einsum('pq,aqe->ape', stiffness, values, precision=HI)
        local = local + jnp.einsum('pq,aqe->ape', curl_matrix, evals, precision=HI)
        local = jnp.where(valid, local, 0.0)
        return jnp.zeros((6, NODES), jnp.float32).at[:, where_node].add(local)

    assembled = lax.map(one_mode, (field, emf))
    wall_node = (jnp.arange(WALL, dtype=jnp.int32) // WALL_DEV) * NODES_DEV + wall_index
    trace = field[:, jnp.array([2, 5])][:, :, wall_node].astype(jnp.bfloat16)

    def one_flux(pair):
        mat, tr = pair
        return jnp.dot(tr.astype(jnp.float32), mat.astype(jnp.float32).T, precision=HI)

    flux = lax.map(one_flux, (dtn, trace))
    coef = (jnp.arange(MODES, dtype=jnp.float32) / MODES) ** 2
    total = assembled - 4.0 * coef[:, None, None] * mass[None, None, :] * field
    total = total.at[:, 2, wall_node].add(-0.5 * flux[:, 0])
    total = total.at[:, 5, wall_node].add(-0.5 * flux[:, 1])
    return total / mass[None, None, :], flux


def reference(field, velocity, stiffness, curl_matrix, mass, connect, wall_index, dtn):
    args = (velocity, stiffness, curl_matrix, mass, connect, wall_index, dtn)
    first, flux_one = rate(field, *args)
    section = field + 0.2 * first
    second, flux_two = rate(section, *args)
    return 0.5 * (field + section + 0.2 * second), jnp.stack([flux_one, flux_two])
```

```python
import functools

import jax
import jax.numpy as jnp
import numpy as np
from jax import lax
from jax.experimental import pallas as pl
from jax.experimental.pallas import tpu as pltpu
from jax.sharding import PartitionSpec as P

GHOST = 256
PAD = 8
MESH = pl.DeviceIdType.MESH
BF = jnp.bfloat16
F32 = jnp.float32


def transforms(modes, nphi):
    angle = 2.0 * np.pi * ((np.arange(modes)[:, None] * np.arange(nphi)[None, :]) % nphi) / nphi
    table = np.stack([np.cos(angle), -np.sin(angle)], 1)
    forward = np.zeros((3, nphi, modes, PAD))
    inverse = np.zeros((modes, PAD, 3, nphi))
    for p in range(2):
        for c in range(3):
            forward[c, :, :, 3 * p + c] = table[:, p].T
            inverse[:, 3 * p + c, (c - 1) % 3, :] = table[:, p] / nphi
    forward = forward.reshape(3 * nphi, modes * PAD)
    inverse = inverse.reshape(modes * PAD, 3 * nphi)
    return jnp.asarray(forward, BF), jnp.asarray(inverse, BF)


def mm(a, b):
    return jnp.dot(a, b, preferred_element_type=F32)


def mm_t(a, b):
    return lax.dot_general(a, b, (((1,), (1,)), ((), ())), preferred_element_type=F32)


def onehot(hit):
    return jnp.where(hit, 1.0, 0.0).astype(BF)


def iota(shape, dim):
    return lax.broadcasted_iota(jnp.int32, shape, dim)


def kernel(
    n_mode,
    n_mer,
    modes,
    field_ref,
    vel_ref,
    stiff_ref,
    curl_ref,
    mass_ref,
    connect_ref,
    wall_ref,
    dtn_ref,
    forward_ref,
    inverse_ref,
    out_ref,
    flux_ref,
    f_full,
    f_part,
    f_got,
    f_prev,
    f_next,
    e_part,
    e_own,
    e_prev,
    e_next,
    t_part,
    t_got,
    c_prev,
    kmat,
    pick,
    oper,
    wall_hot,
    send_sem,
    recv_sem,
):
    mode_dev, _, nodes = field_ref.shape
    nphi = vel_ref.shape[1]
    rows = mode_dev * PAD
    chunk = nodes // n_mode
    ghosts = GHOST // chunk
    elems, npe = connect_ref.shape
    wall_dev = wall_ref.shape[1]
    slots = elems * npe
    ext = nodes + GHOST
    me = lax.axis_index("mode")
    d = lax.axis_index("mer")
    has_prev = d > 0
    has_next = d < n_mer - 1

    def at(mode, mer):
        return {"mode": mode, "mer": mer}

    def other_mode(k):
        return lax.rem(me + k, n_mode)

    def other_mer(k):
        return lax.rem(d + k, n_mer)

    barrier = pltpu.get_barrier_semaphore()

    def greet(mode, mer):
        pl.semaphore_signal(barrier, inc=1, device_id=at(mode, mer), device_id_type=MESH)

    for k in range(1, n_mode):
        greet(other_mode(k), d)

    @pl.when(has_prev)
    def _():
        for k in range(n_mode):
            greet(other_mode(k), d - 1)

    @pl.when(has_next)
    def _():
        for k in range(n_mode):
            greet(other_mode(k), d + 1)

    for k in range(1, n_mer):
        peer = other_mer(k)

        @pl.when(jnp.logical_and(peer != d - 1, peer != d + 1))
        def _():
            greet(me, peer)

    s_f = 0
    s_eo = s_f + n_mode
    s_ep = s_eo + n_mode
    s_en = s_ep + n_mode
    s_fp = s_en + n_mode
    s_fn = s_fp + 1
    s_t = s_fn + 1
    s_c = s_t + n_mer

    def copy(src, dst, sec, out_no, in_no, mode, mer):
        return pltpu.make_async_remote_copy(
            src_ref=src,
            dst_ref=dst,
            send_sem=send_sem.at[sec, out_no],
            recv_sem=recv_sem.at[sec, in_no],
            device_id=at(mode, mer),
            device_id_type=MESH,
        )

    def f_copies(sec):
        return [
            copy(f_part.at[sec, other_mode(k)], f_got.at[sec, me], sec, s_f + other_mode(k), s_f + me, other_mode(k), d)
            for k in range(1, n_mode)
        ]

    def t_copies(sec):
        return [
            copy(t_part.at[sec], t_got.at[sec, d], sec, s_t + other_mer(k), s_t + d, me, other_mer(k))
            for k in range(1, n_mer)
        ]

    def up_copies(sec):
        made = [copy(f_full.at[sec], f_prev.at[sec], sec, s_fp, s_fp, me, d + 1)]
        if sec == 0:
            made.append(copy(connect_ref, c_prev, sec, s_c, s_c, me, d + 1))
        return made

    def down_copies(sec):
        return [copy(f_full.at[sec, :, pl.ds(0, GHOST)], f_next.at[sec], sec, s_fn, s_fn, me, d - 1)]

    def e_copies(sec):
        return [
            copy(e_part.at[sec, other_mode(k)], e_own.at[sec, me], sec, s_eo + other_mode(k), s_eo + me, other_mode(k), d)
            for k in range(1, n_mode)
        ]

    def e_up_copies(sec):
        return [
            copy(e_part.at[sec, other_mode(k)], e_prev.at[sec, me], sec, s_ep + other_mode(k), s_ep + me, other_mode(k), d + 1)
            for k in range(n_mode)
        ]

    def e_down_copies(sec):
        return [
            copy(e_part.at[sec, other_mode(k)], e_next.at[sec, me], sec, s_en + other_mode(k), s_en + me, other_mode(k), d - 1)
            for k in range(n_mode)
        ]

    sends_down = jnp.logical_and(has_prev, me < ghosts)

    def start(copies):
        for c in copies:
            c.start()

    def sent(copies):
        for c in copies:
            c.wait_send()

    def arrive(ref, sec, no):
        copy(ref, ref, sec, no, no, me, d).wait_recv()

    field = jnp.concatenate(
        [
            part
            for m in range(mode_dev)
            for part in (field_ref[m], jnp.zeros((PAD - 6, nodes), F32))
        ],
        0,
    )
    halves = 128 // wall_dev
    wall_row = jnp.concatenate([wall_ref[...]] * halves, 1)
    lane = iota((1, 128), 1)
    wall_row = jnp.where(lane // wall_dev == lax.rem(d, halves), wall_row, -1)
    wall_hot[...] = onehot(iota((nodes, 128), 0) == wall_row)

    take_row = iota((2 * mode_dev, rows), 0)
    take = onehot(iota((2 * mode_dev, rows), 1) == (take_row // 2) * PAD + 2 + 3 * (take_row % 2))
    put_row = iota((rows, 2 * mode_dev), 1)
    put = onehot(iota((rows, 2 * mode_dev), 0) == (put_row // 2) * PAD + 2 + 3 * (put_row % 2))

    def stage(sec, value):
        low = value.astype(BF)
        f_full[sec] = low
        for j in range(n_mode):
            f_part[sec, j] = low[:, j * chunk : (j + 1) * chunk]
        f_got[sec, me] = f_part[sec, me]

    def stage_trace(sec):
        walls = mm(mm(take, f_full[sec]).astype(BF), wall_hot[...]).astype(BF)
        t_part[sec] = walls
        t_got[sec, d] = walls

    def send_field(sec):
        start(f_copies(sec))

        @pl.when(has_next)
        def _():
            start(up_copies(sec))

        @pl.when(has_prev)
        def _():
            start(down_copies(sec))

    stage(0, field)

    @pl.when(jnp.logical_not(has_prev))
    def _():
        f_prev[...] = jnp.zeros(f_prev.shape, BF)
        e_prev[...] = jnp.zeros(e_prev.shape, BF)
        c_prev[...] = jnp.full(c_prev.shape, -1, jnp.int32)

    @pl.when(jnp.logical_not(has_next))
    def _():
        f_next[...] = jnp.zeros(f_next.shape, BF)
        e_next[...] = jnp.zeros(e_next.shape, BF)

    prev_n = has_prev.astype(jnp.int32)
    next_n = has_next.astype(jnp.int32)
    pl.semaphore_wait(barrier, n_mode - 1 + n_mer - 1 + (n_mode - 1) * (prev_n + next_n))

    send_field(0)
    stage_trace(0)
    start(t_copies(0))

    group = 256 // npe
    same = iota((256, 256), 0) // npe == iota((256, 256), 1) // npe

    def spread(ref, sign):
        wide = jnp.concatenate([sign * ref[...]] * group, 1)
        return jnp.where(same, jnp.concatenate([wide] * group, 0), 0.0).astype(BF)

    kmat[0] = spread(stiff_ref, -1.0)
    kmat[1] = spread(curl_ref, 1.0)
    blocks = nodes // 256
    step = 128

    def fill_pick(ref):
        numbers = jnp.concatenate([ref[e : e + 1, :] for e in range(elems)], 1)

        def fill(i, carry):
            base = pl.multiple_of(i * step, step)
            pick[pl.ds(base, step), :] = onehot(iota((step, slots), 0) + base == numbers)
            return carry

        lax.fori_loop(0, ext // step, fill, 0)

    def build(index, first, which):
        take_rows = pick[pl.ds(pl.multiple_of(first, 256), 256), :]
        moved = jnp.concatenate(
            [mm(take_rows[:, g * 256 : (g + 1) * 256], kmat[which]).astype(BF) for g in range(slots // 256)], 1
        )
        oper[index] = mm_t(pick[...], moved).astype(BF)

    def build_own(i, carry):
        build(i, lax.rem(i, blocks) * 256, i // blocks)
        return carry

    def build_prev(i, carry):
        build(2 * blocks + i, nodes, i)
        return carry

    fill_pick(connect_ref)
    lax.fori_loop(0, 2 * blocks, build_own, 0)

    mass_inv = 1.0 / mass_ref[...]
    mode_no = me * mode_dev + iota((rows, 1), 0) // PAD
    damp = 4.0 * (mode_no.astype(F32) / modes) ** 2

    def apply(own, nxt, prv, which):
        here = jnp.concatenate([own, nxt], 1)
        sums = [mm(here, oper[which * blocks + b]) for b in range(blocks)]
        sums[0] = sums[0] + mm(jnp.concatenate([prv, own[:, :GHOST]], 1), oper[2 * blocks + which])
        return jnp.concatenate(sums, 1)

    def lanes(ref, sec, count):
        return jnp.concatenate([ref[sec, j] for j in range(count)], 1)

    def rate(sec, value):
        for k in range(1, n_mode):
            arrive(f_got.at[sec, other_mode(k)], sec, s_f + other_mode(k))
        phys = mm(forward_ref[...], f_got[sec].reshape(n_mode * rows, chunk))
        px, py, pz = [phys[c * nphi : (c + 1) * nphi] for c in range(3)]
        vx, vy, vz = [vel_ref[c].astype(F32) for c in range(3)]
        cross = jnp.concatenate([vy * pz - vz * py, vz * px - vx * pz, vx * py - vy * px], 0)
        emf = mm(inverse_ref[...], cross.astype(BF)).astype(BF)
        e_part[sec] = emf.reshape(n_mode, rows, chunk)
        e_own[sec, me] = e_part[sec, me]
        start(e_copies(sec))

        @pl.when(has_next)
        def _():
            start(e_up_copies(sec))

        @pl.when(sends_down)
        def _():
            start(e_down_copies(sec))

        if sec == 0:

            @pl.when(has_prev)
            def _():
                arrive(c_prev, sec, s_c)

            fill_pick(c_prev)
            lax.fori_loop(0, 2, build_prev, 0)

        @pl.when(has_prev)
        def _():
            arrive(f_prev.at[sec], sec, s_fp)

        @pl.when(has_next)
        def _():
            arrive(f_next.at[sec], sec, s_fn)

        total = apply(f_full[sec], f_next[sec], f_prev[sec], 0)

        for k in range(1, n_mer):
            arrive(t_got.at[sec, other_mer(k)], sec, s_t + other_mer(k))
        trace = jnp.concatenate(
            [sum([t_got[sec, i + h] for h in range(1, halves)], t_got[sec, i]) for i in range(0, n_mer, halves)], 1
        )
        wide = mm_t(trace, dtn_ref[...].reshape(mode_dev * wall_dev, trace.shape[1]))
        wide = jnp.where(iota(wide.shape, 1) // wall_dev == iota(wide.shape, 0) // 2, wide, 0.0)
        folded = sum([wide[:, i : i + 128] for i in range(128, wide.shape[1], 128)], wide[:, :128])
        flux = sum([folded[:, h * wall_dev : (h + 1) * wall_dev] for h in range(1, halves)], folded[:, :wall_dev])
        for m in range(mode_dev):
            flux_ref[sec, m] = flux[2 * m : 2 * m + 2]
        spots = mm_t(jnp.concatenate([-0.5 * flux] * halves, 1).astype(BF), wall_hot[...])
        total = total + mm(put, spots.astype(BF))

        for k in range(1, n_mode):
            arrive(e_own.at[sec, other_mode(k)], sec, s_eo + other_mode(k))

        @pl.when(has_prev)
        def _():
            for j in range(n_mode):
                arrive(e_prev.at[sec, j], sec, s_ep + j)

        @pl.when(has_next)
        def _():
            for j in range(ghosts):
                arrive(e_next.at[sec, j], sec, s_en + j)

        total = total + apply(lanes(e_own, sec, n_mode), lanes(e_next, sec, ghosts), lanes(e_prev, sec, n_mode), 1)
        return total * mass_inv - damp * value

    section = field + 0.2 * rate(0, field)
    stage(1, section)
    send_field(1)
    stage_trace(1)
    start(t_copies(1))
    second = rate(1, section)
    advanced = 0.5 * (field + section + 0.2 * second)
    for m in range(mode_dev):
        out_ref[m] = advanced[m * PAD : m * PAD + 6]

    for sec in range(2):
        sent(f_copies(sec))
        sent(t_copies(sec))
        sent(e_copies(sec))

        @pl.when(has_next)
        def _():
            sent(up_copies(sec))
            sent(e_up_copies(sec))

        @pl.when(has_prev)
        def _():
            sent(down_copies(sec))

        @pl.when(sends_down)
        def _():
            sent(e_down_copies(sec))


def body(field, velocity, stiffness, curl_matrix, mass, connect, wall_index, dtn):
    n_mode = lax.axis_size("mode")
    n_mer = lax.axis_size("mer")
    mode_dev, _, nodes = field.shape
    modes = mode_dev * n_mode
    nphi = velocity.shape[1]
    elems, npe = connect.shape
    wall_dev = wall_index.shape[0]
    rows = mode_dev * PAD
    chunk = nodes // n_mode
    ghosts = GHOST // chunk
    forward, inverse = transforms(modes, nphi)
    sems = 4 * n_mode + n_mer + 3
    vmem = pl.BlockSpec(memory_space=pltpu.VMEM)
    return pl.pallas_call(
        functools.partial(kernel, n_mode, n_mer, modes),
        out_shape=(
            jax.ShapeDtypeStruct(field.shape, F32),
            jax.ShapeDtypeStruct((2, mode_dev, 2, wall_dev), F32),
        ),
        in_specs=[vmem] * 10,
        out_specs=(vmem, vmem),
        scratch_shapes=[
            pltpu.VMEM((2, rows, nodes), BF),
            pltpu.VMEM((2, n_mode, rows, chunk), BF),
            pltpu.VMEM((2, n_mode, rows, chunk), BF),
            pltpu.VMEM((2, rows, nodes), BF),
            pltpu.VMEM((2, rows, GHOST), BF),
            pltpu.VMEM((2, n_mode, rows, chunk), BF),
            pltpu.VMEM((2, n_mode, rows, chunk), BF),
            pltpu.VMEM((2, n_mode, rows, chunk), BF),
            pltpu.VMEM((2, ghosts, rows, chunk), BF),
            pltpu.VMEM((2, 2 * mode_dev, 128), BF),
            pltpu.VMEM((2, n_mer, 2 * mode_dev, 128), BF),
            pltpu.VMEM((elems, npe), jnp.int32),
            pltpu.VMEM((2, 256, 256), BF),
            pltpu.VMEM((nodes + GHOST, elems * npe), BF),
            pltpu.VMEM((2 * (nodes // 256) + 2, nodes + GHOST, 256), BF),
            pltpu.VMEM((nodes, 128), BF),
            pltpu.SemaphoreType.DMA((2, sems)),
            pltpu.SemaphoreType.DMA((2, sems)),
        ],
        compiler_params=pltpu.CompilerParams(
            collective_id=0, has_side_effects=True, vmem_limit_bytes=40 * 1024 * 1024
        ),
    )(
        field,
        velocity,
        stiffness,
        curl_matrix,
        mass.reshape(1, nodes),
        connect,
        wall_index.reshape(1, wall_dev),
        dtn,
        forward,
        inverse,
    )


def solution(mesh):
    placed = (
        P("mode", None, "mer"),
        P(None, None, ("mer", "mode")),
        P(),
        P(),
        P("mer"),
        P("mer", None),
        P("mer"),
        P("mode", "mer", None),
    )
    return jax.shard_map(
        body,
        mesh=mesh,
        in_specs=placed,
        out_specs=(P("mode", None, "mer"), P(None, "mode", None, "mer")),
        check_vma=False,
    )
```

```python
import functools

import jax
import jax.numpy as jnp
import numpy as np
from jax import lax
from jax.experimental import pallas as pl
from jax.experimental.pallas import tpu as pltpu
from jax.sharding import PartitionSpec as P

GHOST = 256
MESH = pl.DeviceIdType.MESH
BF = jnp.bfloat16
F32 = jnp.float32


def transforms(modes, mode_dev, nphi):
    angle = 2.0 * np.pi * ((np.arange(modes)[:, None] * np.arange(nphi)[None, :]) % nphi) / nphi
    table = np.stack([np.cos(angle), -np.sin(angle)], 1)
    forward = np.zeros((3, nphi, modes, 6))
    inverse = np.zeros((modes, 6, 3, nphi))
    for p in range(2):
        for c in range(3):
            forward[c, :, :, 3 * p + c] = table[:, p].T
            inverse[:, 3 * p + c, (c - 1) % 3, :] = table[:, p] / nphi
    owners = modes // mode_dev
    forward = forward.reshape(3 * nphi, owners, mode_dev, 6).transpose(0, 1, 3, 2).reshape(3 * nphi, modes * 6)
    inverse = inverse.reshape(owners, mode_dev, 6, 3 * nphi).transpose(0, 2, 1, 3).reshape(modes * 6, 3 * nphi)
    return jnp.asarray(forward, F32), jnp.asarray(inverse, F32)


def mm(a, b):
    return jnp.dot(a, b, preferred_element_type=F32)


def mm_t(a, b):
    return lax.dot_general(a, b, (((1,), (1,)), ((), ())), preferred_element_type=F32)


def onehot(hit):
    return jnp.where(hit, 1.0, 0.0).astype(BF)


def iota(shape, dim):
    return lax.broadcasted_iota(jnp.int32, shape, dim)


def kernel(
    n_mode,
    n_mer,
    modes,
    field_in,
    vel_in,
    stiff_in,
    curl_in,
    mass_in,
    connect_in,
    wall_in,
    dtn_in,
    forward_in,
    inverse_in,
    out_ref,
    flux_ref,
    f_full,
    f_part,
    f_got,
    f_prev,
    f_next,
    e_part,
    e_own,
    e_prev,
    e_next,
    t_part,
    t_got,
    c_prev,
    kmat,
    pick,
    wall_hot,
    field_ref,
    vel_ref,
    stiff_ref,
    curl_ref,
    mass_ref,
    connect_ref,
    wall_ref,
    dtn_ref,
    forward_ref,
    inverse_ref,
    send_sem,
    recv_sem,
    load_sem,
):
    _, mode_dev, nodes = field_ref.shape
    nphi = vel_ref.shape[1]
    rows = mode_dev * 6
    chunk = nodes // n_mode
    ghosts = GHOST // chunk
    elems, npe = connect_ref.shape
    wall_dev = wall_ref.shape[1]
    slots = elems * npe
    ext = nodes + GHOST
    me = lax.axis_index("mode")
    d = lax.axis_index("mer")
    has_prev = d > 0
    has_next = d < n_mer - 1

    def at(mode, mer):
        return {"mode": mode, "mer": mer}

    def other_mode(k):
        return lax.rem(me + k, n_mode)

    def other_mer(k):
        return lax.rem(d + k, n_mer)

    loads = [
        pltpu.make_async_copy(src, dst, load_sem.at[i])
        for i, (src, dst) in enumerate(
            [
                (field_in, field_ref),
                (connect_in, connect_ref),
                (wall_in, wall_ref),
                (stiff_in, stiff_ref),
                (curl_in, curl_ref),
                (forward_in, forward_ref),
                (vel_in, vel_ref),
                (inverse_in, inverse_ref),
                (dtn_in, dtn_ref),
                (mass_in, mass_ref),
            ]
        )
    ]
    for load in loads:
        load.start()

    barrier = pltpu.get_barrier_semaphore()

    def greet(mode, mer):
        pl.semaphore_signal(barrier, inc=1, device_id=at(mode, mer), device_id_type=MESH)

    for k in range(1, n_mode):
        greet(other_mode(k), d)

    @pl.when(has_prev)
    def _():
        for k in range(n_mode):
            greet(other_mode(k), d - 1)

    @pl.when(has_next)
    def _():
        for k in range(n_mode):
            greet(other_mode(k), d + 1)

    for k in range(1, n_mer):
        peer = other_mer(k)

        @pl.when(jnp.logical_and(peer != d - 1, peer != d + 1))
        def _():
            greet(me, peer)

    s_f = 0
    s_eo = s_f + n_mode
    s_ep = s_eo + n_mode
    s_en = s_ep + n_mode
    s_fp = s_en + n_mode
    s_fn = s_fp + 1
    s_t = s_fn + 1
    s_c = s_t + n_mer

    def copy(src, dst, sec, out_no, in_no, mode, mer):
        return pltpu.make_async_remote_copy(
            src_ref=src,
            dst_ref=dst,
            send_sem=send_sem.at[sec, out_no],
            recv_sem=recv_sem.at[sec, in_no],
            device_id=at(mode, mer),
            device_id_type=MESH,
        )

    def f_copies(sec):
        return [
            copy(f_part.at[sec, other_mode(k)], f_got.at[sec, me], sec, s_f + other_mode(k), s_f + me, other_mode(k), d)
            for k in range(1, n_mode)
        ]

    def t_copies(sec):
        return [
            copy(t_part.at[sec], t_got.at[sec, d], sec, s_t + other_mer(k), s_t + d, me, other_mer(k))
            for k in range(1, n_mer)
        ]

    def up_copies(sec):
        made = [copy(f_full.at[sec], f_prev.at[sec], sec, s_fp, s_fp, me, d + 1)]
        if sec == 0:
            made.append(copy(connect_ref, c_prev, sec, s_c, s_c, me, d + 1))
        return made

    def down_copies(sec):
        return [copy(f_full.at[sec, :, pl.ds(0, GHOST)], f_next.at[sec], sec, s_fn, s_fn, me, d - 1)]

    def e_copies(sec):
        return [
            copy(e_part.at[sec, other_mode(k)], e_own.at[sec, me], sec, s_eo + other_mode(k), s_eo + me, other_mode(k), d)
            for k in range(1, n_mode)
        ]

    def e_up_copies(sec):
        return [
            copy(e_part.at[sec, other_mode(k)], e_prev.at[sec, me], sec, s_ep + other_mode(k), s_ep + me, other_mode(k), d + 1)
            for k in range(n_mode)
        ]

    def e_down_copies(sec):
        return [
            copy(e_part.at[sec, other_mode(k)], e_next.at[sec, me], sec, s_en + other_mode(k), s_en + me, other_mode(k), d - 1)
            for k in range(n_mode)
        ]

    sends_down = jnp.logical_and(has_prev, me < ghosts)

    def start(copies):
        for c in copies:
            c.start()

    def sent(copies):
        for c in copies:
            c.wait_send()

    def arrive(ref, sec, no):
        copy(ref, ref, sec, no, no, me, d).wait_recv()

    halves = 128 // wall_dev

    def stage(sec, value):
        low = value.astype(BF)
        f_full[sec] = low
        for j in range(n_mode):
            f_part[sec, j] = low[:, j * chunk : (j + 1) * chunk]
        f_got[sec, me] = f_part[sec, me]

    def stage_trace(sec):
        low = f_full[sec]
        picked = jnp.concatenate([low[r * mode_dev : (r + 1) * mode_dev] for r in (2, 5)], 0)
        walls = mm(picked, wall_hot[...]).astype(BF)
        t_part[sec] = walls
        t_got[sec, d] = walls

    def send_field(sec):
        start(f_copies(sec))

        @pl.when(has_next)
        def _():
            start(up_copies(sec))

        @pl.when(has_prev)
        def _():
            start(down_copies(sec))

    loads[0].wait()
    field = field_ref[...].reshape(rows, nodes)
    stage(0, field)

    @pl.when(jnp.logical_not(has_prev))
    def _():
        f_prev[...] = jnp.zeros(f_prev.shape, BF)
        e_prev[...] = jnp.zeros(e_prev.shape, BF)
        c_prev[...] = jnp.full(c_prev.shape, -1, jnp.int32)

    @pl.when(jnp.logical_not(has_next))
    def _():
        f_next[...] = jnp.zeros(f_next.shape, BF)
        e_next[...] = jnp.zeros(e_next.shape, BF)

    prev_n = has_prev.astype(jnp.int32)
    next_n = has_next.astype(jnp.int32)
    pl.semaphore_wait(barrier, n_mode - 1 + n_mer - 1 + (n_mode - 1) * (prev_n + next_n))

    loads[1].wait()
    send_field(0)

    step = 128

    def fill_pick(which, ref):
        numbers = jnp.concatenate([ref[e : e + 1, :] for e in range(elems)], 1)

        def fill(i, carry):
            base = pl.multiple_of(i * step, step)
            pick[which, pl.ds(base, step), :] = onehot(iota((step, slots), 0) + base == numbers)
            return carry

        lax.fori_loop(0, ext // step, fill, 0)

    loads[2].wait()
    wall_row = jnp.concatenate([wall_ref[...]] * halves, 1)
    lane = iota((1, 128), 1)
    wall_row = jnp.where(lane // wall_dev == lax.rem(d, halves), wall_row, -1)
    wall_hot[...] = onehot(iota((nodes, 128), 0) == wall_row)
    stage_trace(0)
    start(t_copies(0))

    fill_pick(0, connect_ref)

    wide_dim = 256
    group = wide_dim // npe
    groups = slots // wide_dim
    same = iota((wide_dim, wide_dim), 0) // npe == iota((wide_dim, wide_dim), 1) // npe

    def spread(ref, sign):
        turned = jnp.concatenate([sign * ref[...].T] * group, 1)
        return jnp.where(same, jnp.concatenate([turned] * group, 0), 0.0).astype(BF)

    loads[3].wait()
    kmat[0] = spread(stiff_ref, -1.0)
    loads[4].wait()
    kmat[1] = spread(curl_ref, 1.0)

    for load in loads[5:]:
        load.wait()
    mass_inv = 1.0 / mass_ref[...]
    mode_no = me * mode_dev + lax.rem(iota((rows, 1), 0), mode_dev)
    damp = 4.0 * (mode_no.astype(F32) / modes) ** 2

    def local(own, nxt, prv, which):
        here = mm(jnp.concatenate([own, nxt], 1), pick[0]).astype(BF)
        back = mm(jnp.concatenate([prv, own[:, :GHOST]], 1), pick[1]).astype(BF)
        tall = jnp.concatenate(
            [x[:, g * wide_dim : (g + 1) * wide_dim] for x in (here, back) for g in range(groups)], 0
        )
        done = mm(tall, kmat[which])
        return [done[i * rows : (i + 1) * rows] for i in range(2 * groups)]

    def scatter(parts):
        low = [x.astype(BF) for x in parts]
        total = mm_t(jnp.concatenate(low[:groups], 1), pick[0, :nodes, :])
        extra = mm_t(jnp.concatenate(low[groups:], 1), pick[1, nodes:, :])
        return jnp.concatenate([total[:, :GHOST] + extra, total[:, GHOST:]], 1)

    def lanes(ref, sec, count):
        return jnp.concatenate([ref[sec, j] for j in range(count)], 1)

    def rate(sec, value):
        for k in range(1, n_mode):
            arrive(f_got.at[sec, other_mode(k)], sec, s_f + other_mode(k))
        phys = mm(forward_ref[...].astype(BF), f_got[sec].reshape(n_mode * rows, chunk))
        px, py, pz = [phys[c * nphi : (c + 1) * nphi] for c in range(3)]
        vx, vy, vz = [vel_ref[c].astype(F32) for c in range(3)]
        cross = jnp.concatenate([vy * pz - vz * py, vz * px - vx * pz, vx * py - vy * px], 0)
        emf = mm(inverse_ref[...].astype(BF), cross.astype(BF)).astype(BF)
        e_part[sec] = emf.reshape(n_mode, rows, chunk)
        e_own[sec, me] = e_part[sec, me]
        start(e_copies(sec))

        @pl.when(has_next)
        def _():
            start(e_up_copies(sec))

        @pl.when(sends_down)
        def _():
            start(e_down_copies(sec))

        if sec == 0:

            @pl.when(has_prev)
            def _():
                arrive(c_prev, sec, s_c)

            fill_pick(1, c_prev)

        @pl.when(has_prev)
        def _():
            arrive(f_prev.at[sec], sec, s_fp)

        @pl.when(has_next)
        def _():
            arrive(f_next.at[sec], sec, s_fn)

        diffused = local(f_full[sec], f_next[sec], f_prev[sec], 0)

        for k in range(1, n_mer):
            arrive(t_got.at[sec, other_mer(k)], sec, s_t + other_mer(k))
        trace = jnp.concatenate(
            [sum([t_got[sec, i + h] for h in range(1, halves)], t_got[sec, i]) for i in range(0, n_mer, halves)], 1
        )
        wide = mm_t(trace, dtn_ref[...].reshape(mode_dev * wall_dev, trace.shape[1]))
        wide = jnp.where(iota(wide.shape, 1) // wall_dev == lax.rem(iota(wide.shape, 0), mode_dev), wide, 0.0)
        folded = sum([wide[:, i : i + 128] for i in range(128, wide.shape[1], 128)], wide[:, :128])
        flux = sum([folded[:, h * wall_dev : (h + 1) * wall_dev] for h in range(1, halves)], folded[:, :wall_dev])
        for m in range(mode_dev):
            flux_ref[sec, m] = jnp.concatenate([flux[m : m + 1], flux[mode_dev + m : mode_dev + m + 1]], 0)
        spots = mm_t(jnp.concatenate([-0.5 * flux] * halves, 1).astype(BF), wall_hot[...])
        blank = jnp.zeros((2 * mode_dev, nodes), F32)
        pulled = jnp.concatenate([blank, spots[:mode_dev], blank, spots[mode_dev:]], 0)

        for k in range(1, n_mode):
            arrive(e_own.at[sec, other_mode(k)], sec, s_eo + other_mode(k))

        @pl.when(has_prev)
        def _():
            for j in range(n_mode):
                arrive(e_prev.at[sec, j], sec, s_ep + j)

        @pl.when(has_next)
        def _():
            for j in range(ghosts):
                arrive(e_next.at[sec, j], sec, s_en + j)

        curled = local(lanes(e_own, sec, n_mode), lanes(e_next, sec, ghosts), lanes(e_prev, sec, n_mode), 1)
        total = scatter([x + y for x, y in zip(diffused, curled)]) + pulled
        return total * mass_inv - damp * value

    section = field + 0.2 * rate(0, field)
    stage(1, section)
    send_field(1)
    stage_trace(1)
    start(t_copies(1))
    second = rate(1, section)
    advanced = 0.5 * (field + section + 0.2 * second)
    out_ref[...] = advanced.reshape(out_ref.shape)

    for sec in range(2):
        sent(f_copies(sec))
        sent(t_copies(sec))
        sent(e_copies(sec))

        @pl.when(has_next)
        def _():
            sent(up_copies(sec))
            sent(e_up_copies(sec))

        @pl.when(has_prev)
        def _():
            sent(down_copies(sec))

        @pl.when(sends_down)
        def _():
            sent(e_down_copies(sec))


def body(field, velocity, stiffness, curl_matrix, mass, connect, wall_index, dtn):
    n_mode = lax.axis_size("mode")
    n_mer = lax.axis_size("mer")
    mode_dev, _, nodes = field.shape
    modes = mode_dev * n_mode
    nphi = velocity.shape[1]
    elems, npe = connect.shape
    wall_dev = wall_index.shape[0]
    rows = mode_dev * 6
    chunk = nodes // n_mode
    ghosts = GHOST // chunk
    forward, inverse = transforms(modes, mode_dev, nphi)
    sems = 4 * n_mode + n_mer + 3
    vmem = pl.BlockSpec(memory_space=pltpu.VMEM)
    hbm = pl.BlockSpec(memory_space=pltpu.HBM)
    advanced, flux = pl.pallas_call(
        functools.partial(kernel, n_mode, n_mer, modes),
        out_shape=(
            jax.ShapeDtypeStruct((6, mode_dev, nodes), F32),
            jax.ShapeDtypeStruct((2, mode_dev, 2, wall_dev), F32),
        ),
        in_specs=[hbm] * 10,
        out_specs=(vmem, vmem),
        scratch_shapes=[
            pltpu.VMEM((2, rows, nodes), BF),
            pltpu.VMEM((2, n_mode, rows, chunk), BF),
            pltpu.VMEM((2, n_mode, rows, chunk), BF),
            pltpu.VMEM((2, rows, nodes), BF),
            pltpu.VMEM((2, rows, GHOST), BF),
            pltpu.VMEM((2, n_mode, rows, chunk), BF),
            pltpu.VMEM((2, n_mode, rows, chunk), BF),
            pltpu.VMEM((2, n_mode, rows, chunk), BF),
            pltpu.VMEM((2, ghosts, rows, chunk), BF),
            pltpu.VMEM((2, 2 * mode_dev, 128), BF),
            pltpu.VMEM((2, n_mer, 2 * mode_dev, 128), BF),
            pltpu.VMEM((elems, npe), jnp.int32),
            pltpu.VMEM((2, 256, 256), BF),
            pltpu.VMEM((2, nodes + GHOST, elems * npe), BF),
            pltpu.VMEM((nodes, 128), BF),
            pltpu.VMEM((6, mode_dev, nodes), F32),
            pltpu.VMEM(velocity.shape, BF),
            pltpu.VMEM(stiffness.shape, F32),
            pltpu.VMEM(curl_matrix.shape, F32),
            pltpu.VMEM((1, nodes), F32),
            pltpu.VMEM(connect.shape, jnp.int32),
            pltpu.VMEM((1, wall_dev), jnp.int32),
            pltpu.VMEM(dtn.shape, BF),
            pltpu.VMEM(forward.shape, F32),
            pltpu.VMEM(inverse.shape, F32),
            pltpu.SemaphoreType.DMA((2, sems)),
            pltpu.SemaphoreType.DMA((2, sems)),
            pltpu.SemaphoreType.DMA((10,)),
        ],
        compiler_params=pltpu.CompilerParams(
            collective_id=0, has_side_effects=True, vmem_limit_bytes=60 * 1024 * 1024
        ),
    )(
        jnp.swapaxes(field, 0, 1),
        velocity,
        stiffness,
        curl_matrix,
        mass.reshape(1, nodes),
        connect,
        wall_index.reshape(1, wall_dev),
        dtn,
        forward,
        inverse,
    )
    return jnp.swapaxes(advanced, 0, 1), flux


def solution(mesh):
    placed = (
        P("mode", None, "mer"),
        P(None, None, ("mer", "mode")),
        P(),
        P(),
        P("mer"),
        P("mer", None),
        P("mer"),
        P("mode", "mer", None),
    )
    return jax.shard_map(
        body,
        mesh=mesh,
        in_specs=placed,
        out_specs=(P("mode", None, "mer"), P(None, "mode", None, "mer")),
        check_vma=False,
    )
```

```python
import functools

import jax
import jax.numpy as jnp
import numpy as np
from jax import lax
from jax.experimental import pallas as pl
from jax.experimental.pallas import tpu as pltpu
from jax.sharding import PartitionSpec as P

GHOST = 256
MESH = pl.DeviceIdType.MESH
BF = jnp.bfloat16
F32 = jnp.float32


def transforms(modes, mode_dev, nphi):
    angle = 2.0 * np.pi * ((np.arange(modes)[:, None] * np.arange(nphi)[None, :]) % nphi) / nphi
    table = np.stack([np.cos(angle), -np.sin(angle)], 1)
    forward = np.zeros((3, nphi, modes, 6))
    inverse = np.zeros((modes, 6, 3, nphi))
    for p in range(2):
        for c in range(3):
            forward[c, :, :, 3 * p + c] = table[:, p].T
            inverse[:, 3 * p + c, (c - 1) % 3, :] = table[:, p] / nphi
    owners = modes // mode_dev
    forward = forward.reshape(3 * nphi, owners, mode_dev, 6).transpose(0, 1, 3, 2).reshape(3 * nphi, modes * 6)
    inverse = inverse.reshape(owners, mode_dev, 6, 3 * nphi).transpose(0, 2, 1, 3).reshape(modes * 6, 3 * nphi)
    return jnp.asarray(forward, F32), jnp.asarray(inverse, F32)


def mm(a, b):
    return jnp.dot(a, b, preferred_element_type=F32)


def mm_t(a, b):
    return lax.dot_general(a, b, (((1,), (1,)), ((), ())), preferred_element_type=F32)


def onehot(hit):
    return jnp.where(hit, 1.0, 0.0).astype(BF)


def iota(shape, dim):
    return lax.broadcasted_iota(jnp.int32, shape, dim)


def kernel(
    n_mode,
    n_mer,
    modes,
    field_in,
    vel_in,
    stiff_in,
    curl_in,
    mass_in,
    connect_in,
    wall_in,
    dtn_in,
    forward_in,
    inverse_in,
    out_ref,
    flux_ref,
    f_full,
    f_part,
    f_got,
    f_prev,
    f_next,
    e_part,
    e_own,
    e_prev,
    e_next,
    t_part,
    t_got,
    c_prev,
    kmat,
    pick,
    wall_hot,
    field_ref,
    vel_ref,
    stiff_ref,
    curl_ref,
    mass_ref,
    connect_ref,
    wall_ref,
    dtn_ref,
    forward_ref,
    inverse_ref,
    send_sem,
    recv_sem,
    load_sem,
):
    _, mode_dev, nodes = field_ref.shape
    nphi = vel_ref.shape[1]
    rows = mode_dev * 6
    chunk = nodes // n_mode
    ghosts = GHOST // chunk
    elems, npe = connect_ref.shape
    wall_dev = wall_ref.shape[1]
    slots = elems * npe
    ext = nodes + GHOST
    me = lax.axis_index("mode")
    d = lax.axis_index("mer")
    has_prev = d > 0
    has_next = d < n_mer - 1

    def at(mode, mer):
        return {"mode": mode, "mer": mer}

    def other_mode(k):
        return lax.rem(me + k, n_mode)

    def other_mer(k):
        return lax.rem(d + k, n_mer)

    loads = [
        pltpu.make_async_copy(src, dst, load_sem.at[i])
        for i, (src, dst) in enumerate(
            [
                (field_in, field_ref),
                (connect_in, connect_ref),
                (wall_in, wall_ref),
                (stiff_in, stiff_ref),
                (curl_in, curl_ref),
                (forward_in, forward_ref),
                (vel_in, vel_ref),
                (inverse_in, inverse_ref),
                (dtn_in, dtn_ref),
                (mass_in, mass_ref),
            ]
        )
    ]
    loads[0].start()

    barrier = pltpu.get_barrier_semaphore()

    def greet(mode, mer):
        pl.semaphore_signal(barrier, inc=1, device_id=at(mode, mer), device_id_type=MESH)

    for k in range(1, n_mode):
        greet(other_mode(k), d)

    @pl.when(has_prev)
    def _():
        for k in range(n_mode):
            greet(other_mode(k), d - 1)

    @pl.when(has_next)
    def _():
        for k in range(n_mode):
            greet(other_mode(k), d + 1)

    for k in range(1, n_mer):
        peer = other_mer(k)

        @pl.when(jnp.logical_and(peer != d - 1, peer != d + 1))
        def _():
            greet(me, peer)

    for load in loads[1:]:
        load.start()

    s_f = 0
    s_eo = s_f + n_mode
    s_ep = s_eo + n_mode
    s_en = s_ep + n_mode
    s_fp = s_en + n_mode
    s_fn = s_fp + 1
    s_t = s_fn + 1
    s_c = s_t + n_mer

    def copy(src, dst, sec, out_no, in_no, mode, mer):
        return pltpu.make_async_remote_copy(
            src_ref=src,
            dst_ref=dst,
            send_sem=send_sem.at[sec, out_no],
            recv_sem=recv_sem.at[sec, in_no],
            device_id=at(mode, mer),
            device_id_type=MESH,
        )

    def f_copies(sec):
        return [
            copy(f_part.at[sec, other_mode(k)], f_got.at[sec, me], sec, s_f + other_mode(k), s_f + me, other_mode(k), d)
            for k in range(1, n_mode)
        ]

    def t_copies(sec):
        return [
            copy(t_part.at[sec], t_got.at[sec, d], sec, s_t + other_mer(k), s_t + d, me, other_mer(k))
            for k in range(1, n_mer)
        ]

    def up_copies(sec):
        made = [copy(f_full.at[sec], f_prev.at[sec], sec, s_fp, s_fp, me, d + 1)]
        if sec == 0:
            made.append(copy(connect_ref, c_prev, sec, s_c, s_c, me, d + 1))
        return made

    def down_copies(sec):
        return [copy(f_full.at[sec, :, pl.ds(0, GHOST)], f_next.at[sec], sec, s_fn, s_fn, me, d - 1)]

    def e_copies(sec):
        return [
            copy(e_part.at[sec, other_mode(k)], e_own.at[sec, me], sec, s_eo + other_mode(k), s_eo + me, other_mode(k), d)
            for k in range(1, n_mode)
        ]

    def e_up_copies(sec):
        return [
            copy(e_part.at[sec, other_mode(k)], e_prev.at[sec, me], sec, s_ep + other_mode(k), s_ep + me, other_mode(k), d + 1)
            for k in range(n_mode)
        ]

    def e_down_copies(sec):
        return [
            copy(e_part.at[sec, other_mode(k)], e_next.at[sec, me], sec, s_en + other_mode(k), s_en + me, other_mode(k), d - 1)
            for k in range(n_mode)
        ]

    sends_down = jnp.logical_and(has_prev, me < ghosts)

    def start(copies):
        for c in copies:
            c.start()

    def sent(copies):
        for c in copies:
            c.wait_send()

    def arrive(ref, sec, no):
        copy(ref, ref, sec, no, no, me, d).wait_recv()

    halves = 128 // wall_dev

    def stage(sec, value):
        low = value.astype(BF)
        f_full[sec] = low
        for j in range(n_mode):
            f_part[sec, j] = low[:, j * chunk : (j + 1) * chunk]
        f_got[sec, me] = f_part[sec, me]

    def stage_trace(sec):
        low = f_full[sec]
        picked = jnp.concatenate([low[r * mode_dev : (r + 1) * mode_dev] for r in (2, 5)], 0)
        walls = mm(picked, wall_hot[...]).astype(BF)
        t_part[sec] = walls
        t_got[sec, d] = walls

    def send_field(sec):
        start(f_copies(sec))

        @pl.when(has_next)
        def _():
            start(up_copies(sec))

        @pl.when(has_prev)
        def _():
            start(down_copies(sec))

    loads[0].wait()
    field = field_ref[...].reshape(rows, nodes)
    stage(0, field)

    @pl.when(jnp.logical_not(has_prev))
    def _():
        f_prev[...] = jnp.zeros(f_prev.shape, BF)
        e_prev[...] = jnp.zeros(e_prev.shape, BF)
        c_prev[...] = jnp.full(c_prev.shape, -1, jnp.int32)

    @pl.when(jnp.logical_not(has_next))
    def _():
        f_next[...] = jnp.zeros(f_next.shape, BF)
        e_next[...] = jnp.zeros(e_next.shape, BF)

    prev_n = has_prev.astype(jnp.int32)
    next_n = has_next.astype(jnp.int32)
    pl.semaphore_wait(barrier, n_mode - 1 + n_mer - 1 + (n_mode - 1) * (prev_n + next_n))

    loads[1].wait()
    send_field(0)

    step = 128

    def fill_pick(which, ref):
        numbers = jnp.concatenate([ref[e : e + 1, :] for e in range(elems)], 1)

        def fill(i, carry):
            base = pl.multiple_of(i * step, step)
            pick[which, pl.ds(base, step), :] = onehot(iota((step, slots), 0) + base == numbers)
            return carry

        lax.fori_loop(0, ext // step, fill, 0)

    loads[2].wait()
    wall_row = jnp.concatenate([wall_ref[...]] * halves, 1)
    lane = iota((1, 128), 1)
    wall_row = jnp.where(lane // wall_dev == lax.rem(d, halves), wall_row, -1)
    wall_hot[...] = onehot(iota((nodes, 128), 0) == wall_row)
    stage_trace(0)
    start(t_copies(0))

    wide_dim = 256
    group = wide_dim // npe
    groups = slots // wide_dim
    same = iota((wide_dim, wide_dim), 0) // npe == iota((wide_dim, wide_dim), 1) // npe

    def spread(ref, sign):
        turned = jnp.concatenate([sign * ref[...].T] * group, 1)
        return jnp.where(same, jnp.concatenate([turned] * group, 0), 0.0).astype(BF)

    def prepare():
        fill_pick(0, connect_ref)
        loads[3].wait()
        kmat[0] = spread(stiff_ref, -1.0)
        loads[4].wait()
        kmat[1] = spread(curl_ref, 1.0)

        @pl.when(has_prev)
        def _():
            arrive(c_prev, 0, s_c)

        fill_pick(1, c_prev)

    for load in loads[5:]:
        load.wait()
    mass_inv = 1.0 / mass_ref[...]
    mode_no = me * mode_dev + lax.rem(iota((rows, 1), 0), mode_dev)
    damp = 4.0 * (mode_no.astype(F32) / modes) ** 2

    def elements(here, back, which):
        low = (here.astype(BF), back.astype(BF))
        tall = jnp.concatenate([x[:, g * wide_dim : (g + 1) * wide_dim] for x in low for g in range(groups)], 0)
        done = mm(tall, kmat[which])
        return [done[i * rows : (i + 1) * rows] for i in range(2 * groups)]

    def gather_own(own):
        return mm(own, pick[0, :nodes, :]), mm(own[:, :GHOST], pick[1, nodes:, :])

    def gather_next(nxt):
        return mm(nxt, pick[0, nodes:, :])

    def gather_prev(prv):
        return mm(prv, pick[1, :nodes, :])

    def scatter(parts):
        low = [x.astype(BF) for x in parts]
        total = mm_t(jnp.concatenate(low[:groups], 1), pick[0, :nodes, :])
        extra = mm_t(jnp.concatenate(low[groups:], 1), pick[1, nodes:, :])
        return jnp.concatenate([total[:, :GHOST] + extra, total[:, GHOST:]], 1)

    def lanes(ref, sec, count):
        return jnp.concatenate([ref[sec, j] for j in range(count)], 1)

    def all_sent(sec):
        sent(f_copies(sec))
        sent(t_copies(sec))
        sent(e_copies(sec))

        @pl.when(has_next)
        def _():
            sent(up_copies(sec))
            sent(e_up_copies(sec))

        @pl.when(has_prev)
        def _():
            sent(down_copies(sec))

        @pl.when(sends_down)
        def _():
            sent(e_down_copies(sec))

    def rate(sec, value):
        for k in range(1, n_mode):
            arrive(f_got.at[sec, other_mode(k)], sec, s_f + other_mode(k))
        phys = mm(forward_ref[...].astype(BF), f_got[sec].reshape(n_mode * rows, chunk))
        px, py, pz = [phys[c * nphi : (c + 1) * nphi] for c in range(3)]
        vx, vy, vz = [vel_ref[c].astype(F32) for c in range(3)]
        cross = jnp.concatenate([vy * pz - vz * py, vz * px - vx * pz, vx * py - vy * px], 0)
        emf = mm(inverse_ref[...].astype(BF), cross.astype(BF)).astype(BF)
        e_part[sec] = emf.reshape(n_mode, rows, chunk)
        e_own[sec, me] = e_part[sec, me]
        start(e_copies(sec))

        @pl.when(has_next)
        def _():
            start(e_up_copies(sec))

        @pl.when(sends_down)
        def _():
            start(e_down_copies(sec))

        if sec == 0:
            prepare()
        else:
            all_sent(0)

        @pl.when(has_prev)
        def _():
            arrive(f_prev.at[sec], sec, s_fp)

        @pl.when(has_next)
        def _():
            arrive(f_next.at[sec], sec, s_fn)

        here, back = gather_own(f_full[sec])
        diffused = elements(here + gather_next(f_next[sec]), back + gather_prev(f_prev[sec]), 0)

        for k in range(1, n_mer):
            arrive(t_got.at[sec, other_mer(k)], sec, s_t + other_mer(k))
        trace = jnp.concatenate(
            [sum([t_got[sec, i + h] for h in range(1, halves)], t_got[sec, i]) for i in range(0, n_mer, halves)], 1
        )
        wide = mm_t(trace, dtn_ref[...].reshape(mode_dev * wall_dev, trace.shape[1]))
        wide = jnp.where(iota(wide.shape, 1) // wall_dev == lax.rem(iota(wide.shape, 0), mode_dev), wide, 0.0)
        folded = sum([wide[:, i : i + 128] for i in range(128, wide.shape[1], 128)], wide[:, :128])
        flux = sum([folded[:, h * wall_dev : (h + 1) * wall_dev] for h in range(1, halves)], folded[:, :wall_dev])
        for m in range(mode_dev):
            flux_ref[sec, m] = jnp.concatenate([flux[m : m + 1], flux[mode_dev + m : mode_dev + m + 1]], 0)
        spots = mm_t(jnp.concatenate([-0.5 * flux] * halves, 1).astype(BF), wall_hot[...])
        blank = jnp.zeros((2 * mode_dev, nodes), F32)
        pulled = jnp.concatenate([blank, spots[:mode_dev], blank, spots[mode_dev:]], 0)

        for k in range(1, n_mode):
            arrive(e_own.at[sec, other_mode(k)], sec, s_eo + other_mode(k))
        here, back = gather_own(lanes(e_own, sec, n_mode))

        @pl.when(has_prev)
        def _():
            for j in range(n_mode):
                arrive(e_prev.at[sec, j], sec, s_ep + j)

        back = back + gather_prev(lanes(e_prev, sec, n_mode))

        @pl.when(has_next)
        def _():
            for j in range(ghosts):
                arrive(e_next.at[sec, j], sec, s_en + j)

        here = here + gather_next(lanes(e_next, sec, ghosts))
        curled = elements(here, back, 1)
        total = scatter([x + y for x, y in zip(diffused, curled)]) + pulled
        return total * mass_inv - damp * value

    section = field + 0.2 * rate(0, field)
    stage(1, section)
    send_field(1)
    stage_trace(1)
    start(t_copies(1))
    second = rate(1, section)
    advanced = 0.5 * (field + section + 0.2 * second)
    out_ref[...] = advanced.reshape(out_ref.shape)

    all_sent(1)


def finish(out_in, flux_in, out_ref, flux_ref, sem):
    copies = [
        pltpu.make_async_copy(out_in, out_ref, sem.at[0]),
        pltpu.make_async_copy(flux_in, flux_ref, sem.at[1]),
    ]
    for c in copies:
        c.start()
    for c in copies:
        c.wait()


def body(field, velocity, stiffness, curl_matrix, mass, connect, wall_index, dtn):
    n_mode = lax.axis_size("mode")
    n_mer = lax.axis_size("mer")
    mode_dev, _, nodes = field.shape
    modes = mode_dev * n_mode
    nphi = velocity.shape[1]
    elems, npe = connect.shape
    wall_dev = wall_index.shape[0]
    rows = mode_dev * 6
    chunk = nodes // n_mode
    ghosts = GHOST // chunk
    forward, inverse = transforms(modes, mode_dev, nphi)
    sems = 4 * n_mode + n_mer + 3
    vmem = pl.BlockSpec(memory_space=pltpu.VMEM)
    hbm = pl.BlockSpec(memory_space=pltpu.HBM)
    shapes = (
        jax.ShapeDtypeStruct((6, mode_dev, nodes), F32),
        jax.ShapeDtypeStruct((2, mode_dev, 2, wall_dev), F32),
    )
    advanced, flux = pl.pallas_call(
        functools.partial(kernel, n_mode, n_mer, modes),
        out_shape=shapes,
        in_specs=[hbm] * 10,
        out_specs=(vmem, vmem),
        scratch_shapes=[
            pltpu.VMEM((2, rows, nodes), BF),
            pltpu.VMEM((2, n_mode, rows, chunk), BF),
            pltpu.VMEM((2, n_mode, rows, chunk), BF),
            pltpu.VMEM((2, rows, nodes), BF),
            pltpu.VMEM((2, rows, GHOST), BF),
            pltpu.VMEM((2, n_mode, rows, chunk), BF),
            pltpu.VMEM((2, n_mode, rows, chunk), BF),
            pltpu.VMEM((2, n_mode, rows, chunk), BF),
            pltpu.VMEM((2, ghosts, rows, chunk), BF),
            pltpu.VMEM((2, 2 * mode_dev, 128), BF),
            pltpu.VMEM((2, n_mer, 2 * mode_dev, 128), BF),
            pltpu.VMEM((elems, npe), jnp.int32),
            pltpu.VMEM((2, 256, 256), BF),
            pltpu.VMEM((2, nodes + GHOST, elems * npe), BF),
            pltpu.VMEM((nodes, 128), BF),
            pltpu.VMEM((6, mode_dev, nodes), F32),
            pltpu.VMEM(velocity.shape, BF),
            pltpu.VMEM(stiffness.shape, F32),
            pltpu.VMEM(curl_matrix.shape, F32),
            pltpu.VMEM((1, nodes), F32),
            pltpu.VMEM(connect.shape, jnp.int32),
            pltpu.VMEM((1, wall_dev), jnp.int32),
            pltpu.VMEM(dtn.shape, BF),
            pltpu.VMEM(forward.shape, F32),
            pltpu.VMEM(inverse.shape, F32),
            pltpu.SemaphoreType.DMA((2, sems)),
            pltpu.SemaphoreType.DMA((2, sems)),
            pltpu.SemaphoreType.DMA((10,)),
        ],
        compiler_params=pltpu.CompilerParams(
            collective_id=0, has_side_effects=True, vmem_limit_bytes=60 * 1024 * 1024
        ),
    )(
        jnp.swapaxes(field, 0, 1),
        velocity,
        stiffness,
        curl_matrix,
        mass.reshape(1, nodes),
        connect,
        wall_index.reshape(1, wall_dev),
        dtn,
        forward,
        inverse,
    )
    advanced, flux = pl.pallas_call(
        finish,
        out_shape=shapes,
        in_specs=[hbm] * 2,
        out_specs=(hbm, hbm),
        scratch_shapes=[pltpu.SemaphoreType.DMA((2,))],
        compiler_params=pltpu.CompilerParams(vmem_limit_bytes=60 * 1024 * 1024),
    )(advanced, flux)
    return jnp.swapaxes(advanced, 0, 1), flux


def solution(mesh):
    placed = (
        P("mode", None, "mer"),
        P(None, None, ("mer", "mode")),
        P(),
        P(),
        P("mer"),
        P("mer", None),
        P("mer"),
        P("mode", "mer", None),
    )
    return jax.shard_map(
        body,
        mesh=mesh,
        in_specs=placed,
        out_specs=(P("mode", None, "mer"), P(None, "mode", None, "mer")),
        check_vma=False,
    )
```

```python
import functools

import jax
import jax.numpy as jnp
import numpy as np
from jax import lax
from jax.experimental import pallas as pl
from jax.experimental.pallas import tpu as pltpu
from jax.sharding import PartitionSpec as P

GHOST = 256
MESH = pl.DeviceIdType.MESH
BF = jnp.bfloat16
F32 = jnp.float32


def transforms(modes, mode_dev, nphi):
    angle = 2.0 * np.pi * ((np.arange(modes)[:, None] * np.arange(nphi)[None, :]) % nphi) / nphi
    table = np.stack([np.cos(angle), -np.sin(angle)], 1)
    forward = np.zeros((3, nphi, modes, 6))
    inverse = np.zeros((modes, 6, 3, nphi))
    for p in range(2):
        for c in range(3):
            forward[c, :, :, 3 * p + c] = table[:, p].T
            inverse[:, 3 * p + c, (c - 1) % 3, :] = table[:, p] / nphi
    owners = modes // mode_dev
    forward = forward.reshape(3 * nphi, owners, mode_dev, 6).transpose(0, 1, 3, 2).reshape(3 * nphi, modes * 6)
    inverse = inverse.reshape(owners, mode_dev, 6, 3 * nphi).transpose(0, 2, 1, 3).reshape(modes * 6, 3 * nphi)
    return jnp.asarray(forward, F32), jnp.asarray(inverse, F32)


def mm(a, b):
    return jnp.dot(a, b, preferred_element_type=F32)


def mm_t(a, b):
    return lax.dot_general(a, b, (((1,), (1,)), ((), ())), preferred_element_type=F32)


def onehot(hit):
    return jnp.where(hit, 1.0, 0.0).astype(BF)


def iota(shape, dim):
    return lax.broadcasted_iota(jnp.int32, shape, dim)


def kernel(
    n_mode,
    n_mer,
    modes,
    field_in,
    vel_in,
    stiff_in,
    curl_in,
    mass_in,
    connect_in,
    wall_in,
    dtn_in,
    forward_in,
    inverse_in,
    out_ref,
    flux_ref,
    f_full,
    f_part,
    f_got,
    f_prev,
    f_next,
    e_part,
    e_own,
    e_prev,
    e_next,
    t_part,
    t_got,
    c_prev,
    kmat,
    pick,
    wall_hot,
    field_ref,
    vel_ref,
    stiff_ref,
    curl_ref,
    mass_ref,
    connect_ref,
    wall_ref,
    dtn_ref,
    forward_ref,
    inverse_ref,
    send_sem,
    recv_sem,
    load_sem,
):
    _, mode_dev, nodes = field_ref.shape
    nphi = vel_ref.shape[1]
    rows = mode_dev * 6
    chunk = nodes // n_mode
    ghosts = GHOST // chunk
    elems, npe = connect_ref.shape
    wall_dev = wall_ref.shape[1]
    slots = elems * npe
    ext = nodes + GHOST
    me = lax.axis_index("mode")
    d = lax.axis_index("mer")
    has_prev = d > 0
    has_next = d < n_mer - 1

    def at(mode, mer):
        return {"mode": mode, "mer": mer}

    def other_mode(k):
        return lax.rem(me + k, n_mode)

    def other_mer(k):
        return lax.rem(d + k, n_mer)

    loads = [
        pltpu.make_async_copy(src, dst, load_sem.at[i])
        for i, (src, dst) in enumerate(
            [
                (field_in, field_ref),
                (connect_in, connect_ref),
                (wall_in, wall_ref),
                (stiff_in, stiff_ref),
                (curl_in, curl_ref),
                (forward_in, forward_ref),
                (vel_in, vel_ref),
                (inverse_in, inverse_ref),
                (dtn_in, dtn_ref),
                (mass_in, mass_ref),
            ]
        )
    ]
    loads[0].start()

    barrier = pltpu.get_barrier_semaphore()

    def greet(mode, mer):
        pl.semaphore_signal(barrier, inc=1, device_id=at(mode, mer), device_id_type=MESH)

    for k in range(1, n_mode):
        greet(other_mode(k), d)

    @pl.when(has_prev)
    def _():
        for k in range(n_mode):
            greet(other_mode(k), d - 1)

    @pl.when(has_next)
    def _():
        for k in range(n_mode):
            greet(other_mode(k), d + 1)

    for k in range(1, n_mer):
        peer = other_mer(k)

        @pl.when(jnp.logical_and(peer != d - 1, peer != d + 1))
        def _():
            greet(me, peer)

    for load in loads[1:]:
        load.start()

    s_f = 0
    s_eo = s_f + n_mode
    s_ep = s_eo + n_mode
    s_en = s_ep + n_mode
    s_fp = s_en + n_mode
    s_fn = s_fp + 1
    s_t = s_fn + 1
    s_c = s_t + n_mer

    def copy(src, dst, sec, out_no, in_no, mode, mer):
        return pltpu.make_async_remote_copy(
            src_ref=src,
            dst_ref=dst,
            send_sem=send_sem.at[sec, out_no],
            recv_sem=recv_sem.at[sec, in_no],
            device_id=at(mode, mer),
            device_id_type=MESH,
        )

    def f_copies(sec):
        return [
            copy(f_part.at[sec, other_mode(k)], f_got.at[sec, me], sec, s_f + other_mode(k), s_f + me, other_mode(k), d)
            for k in range(1, n_mode)
        ]

    def t_copies(sec):
        return [
            copy(t_part.at[sec], t_got.at[sec, d], sec, s_t + other_mer(k), s_t + d, me, other_mer(k))
            for k in range(1, n_mer)
        ]

    def up_copies(sec):
        return [copy(f_full.at[sec], f_prev.at[sec], sec, s_fp, s_fp, me, d + 1)]

    def connect_copies():
        return [copy(connect_ref, c_prev, 0, s_c, s_c, me, d + 1)]

    def down_copies(sec):
        return [copy(f_full.at[sec, :, pl.ds(0, GHOST)], f_next.at[sec], sec, s_fn, s_fn, me, d - 1)]

    def e_copies(sec):
        return [
            copy(e_part.at[sec, other_mode(k)], e_own.at[sec, me], sec, s_eo + other_mode(k), s_eo + me, other_mode(k), d)
            for k in range(1, n_mode)
        ]

    def e_up_copies(sec):
        return [
            copy(e_part.at[sec, other_mode(k)], e_prev.at[sec, me], sec, s_ep + other_mode(k), s_ep + me, other_mode(k), d + 1)
            for k in range(n_mode)
        ]

    def e_down_copies(sec):
        return [
            copy(e_part.at[sec, other_mode(k)], e_next.at[sec, me], sec, s_en + other_mode(k), s_en + me, other_mode(k), d - 1)
            for k in range(n_mode)
        ]

    sends_down = jnp.logical_and(has_prev, me < ghosts)

    def start(copies):
        for c in copies:
            c.start()

    def sent(copies):
        for c in copies:
            c.wait_send()

    def arrive(ref, sec, no):
        copy(ref, ref, sec, no, no, me, d).wait_recv()

    halves = 128 // wall_dev

    def stage(sec, value):
        low = value.astype(BF)
        f_full[sec] = low
        for j in range(n_mode):
            f_part[sec, j] = low[:, j * chunk : (j + 1) * chunk]
        f_got[sec, me] = f_part[sec, me]

    def stage_trace(sec):
        low = f_full[sec]
        picked = jnp.concatenate([low[r * mode_dev : (r + 1) * mode_dev] for r in (2, 5)], 0)
        walls = mm(picked, wall_hot[...]).astype(BF)
        t_part[sec] = walls
        t_got[sec, d] = walls

    def send_field(sec):
        start(f_copies(sec))

        @pl.when(has_next)
        def _():
            start(up_copies(sec))

        @pl.when(has_prev)
        def _():
            start(down_copies(sec))

    @pl.when(jnp.logical_not(has_prev))
    def _():
        f_prev[...] = jnp.zeros(f_prev.shape, BF)
        e_prev[...] = jnp.zeros(e_prev.shape, BF)
        c_prev[...] = jnp.full(c_prev.shape, -1, jnp.int32)

    @pl.when(jnp.logical_not(has_next))
    def _():
        f_next[...] = jnp.zeros(f_next.shape, BF)
        e_next[...] = jnp.zeros(e_next.shape, BF)

    prev_n = has_prev.astype(jnp.int32)
    next_n = has_next.astype(jnp.int32)
    pl.semaphore_wait(barrier, n_mode - 1 + n_mer - 1 + (n_mode - 1) * (prev_n + next_n))

    loads[0].wait()
    loads[1].wait()

    @pl.when(has_next)
    def _():
        start(connect_copies())

    step = 128

    def fill_pick(which, ref):
        numbers = jnp.concatenate([ref[e : e + 1, :] for e in range(elems)], 1)

        def fill(i, carry):
            base = pl.multiple_of(i * step, step)
            pick[which, pl.ds(base, step), :] = onehot(iota((step, slots), 0) + base == numbers)
            return carry

        lax.fori_loop(0, ext // step, fill, 0)

    loads[2].wait()
    wall_row = jnp.concatenate([wall_ref[...]] * halves, 1)
    lane = iota((1, 128), 1)
    wall_row = jnp.where(lane // wall_dev == lax.rem(d, halves), wall_row, -1)
    wall_hot[...] = onehot(iota((nodes, 128), 0) == wall_row)
    wide_dim = 256
    group = wide_dim // npe
    groups = slots // wide_dim
    same = iota((wide_dim, wide_dim), 0) // npe == iota((wide_dim, wide_dim), 1) // npe

    def spread(ref, sign):
        turned = jnp.concatenate([sign * ref[...].T] * group, 1)
        return jnp.where(same, jnp.concatenate([turned] * group, 0), 0.0).astype(BF)

    def prepare():
        fill_pick(0, connect_ref)
        loads[3].wait()
        kmat[0] = spread(stiff_ref, -1.0)
        loads[4].wait()
        kmat[1] = spread(curl_ref, 1.0)

        @pl.when(has_prev)
        def _():
            arrive(c_prev, 0, s_c)

        @pl.when(has_next)
        def _():
            sent(connect_copies())

        fill_pick(1, c_prev)

    for load in loads[5:]:
        load.wait()
    mass_inv = 1.0 / mass_ref[...]
    mode_no = me * mode_dev + lax.rem(iota((rows, 1), 0), mode_dev)
    damp = 4.0 * (mode_no.astype(F32) / modes) ** 2

    def elements(here, back, which):
        low = (here.astype(BF), back.astype(BF))
        tall = jnp.concatenate([x[:, g * wide_dim : (g + 1) * wide_dim] for x in low for g in range(groups)], 0)
        done = mm(tall, kmat[which])
        return [done[i * rows : (i + 1) * rows] for i in range(2 * groups)]

    def gather_own(own):
        return mm(own, pick[0, :nodes, :]), mm(own[:, :GHOST], pick[1, nodes:, :])

    def gather_next(nxt):
        return mm(nxt, pick[0, nodes:, :])

    def gather_prev(prv):
        return mm(prv, pick[1, :nodes, :])

    def scatter(parts):
        low = [x.astype(BF) for x in parts]
        total = mm_t(jnp.concatenate(low[:groups], 1), pick[0, :nodes, :])
        extra = mm_t(jnp.concatenate(low[groups:], 1), pick[1, nodes:, :])
        return jnp.concatenate([total[:, :GHOST] + extra, total[:, GHOST:]], 1)

    def lanes(ref, sec, count):
        return jnp.concatenate([ref[sec, j] for j in range(count)], 1)

    def field_sent(sec):
        sent(f_copies(sec))
        sent(t_copies(sec))

        @pl.when(has_next)
        def _():
            sent(up_copies(sec))

        @pl.when(has_prev)
        def _():
            sent(down_copies(sec))

    def emf_sent(sec):
        sent(e_copies(sec))

        @pl.when(has_next)
        def _():
            sent(e_up_copies(sec))

        @pl.when(sends_down)
        def _():
            sent(e_down_copies(sec))

    def rate(sec, value):
        for k in range(1, n_mode):
            arrive(f_got.at[sec, other_mode(k)], sec, s_f + other_mode(k))
        phys = mm(forward_ref[...].astype(BF), f_got[sec].reshape(n_mode * rows, chunk))
        px, py, pz = [phys[c * nphi : (c + 1) * nphi] for c in range(3)]
        vx, vy, vz = [vel_ref[c].astype(F32) for c in range(3)]
        cross = jnp.concatenate([vy * pz - vz * py, vz * px - vx * pz, vx * py - vy * px], 0)
        emf = mm(inverse_ref[...].astype(BF), cross.astype(BF)).astype(BF)
        e_part[sec] = emf.reshape(n_mode, rows, chunk)
        e_own[sec, me] = e_part[sec, me]
        start(e_copies(sec))

        @pl.when(has_next)
        def _():
            start(e_up_copies(sec))

        @pl.when(sends_down)
        def _():
            start(e_down_copies(sec))

        @pl.when(sec == 0)
        def _():
            prepare()

        @pl.when(has_prev)
        def _():
            arrive(f_prev.at[sec], sec, s_fp)

        @pl.when(has_next)
        def _():
            arrive(f_next.at[sec], sec, s_fn)

        here, back = gather_own(f_full[sec])
        diffused = elements(here + gather_next(f_next[sec]), back + gather_prev(f_prev[sec]), 0)

        for k in range(1, n_mer):
            arrive(t_got.at[sec, other_mer(k)], sec, s_t + other_mer(k))
        trace = jnp.concatenate(
            [sum([t_got[sec, i + h] for h in range(1, halves)], t_got[sec, i]) for i in range(0, n_mer, halves)], 1
        )
        wide = mm_t(trace, dtn_ref[...].reshape(mode_dev * wall_dev, trace.shape[1]))
        wide = jnp.where(iota(wide.shape, 1) // wall_dev == lax.rem(iota(wide.shape, 0), mode_dev), wide, 0.0)
        folded = sum([wide[:, i : i + 128] for i in range(128, wide.shape[1], 128)], wide[:, :128])
        flux = sum([folded[:, h * wall_dev : (h + 1) * wall_dev] for h in range(1, halves)], folded[:, :wall_dev])
        for m in range(mode_dev):
            flux_ref[sec, m] = jnp.concatenate([flux[m : m + 1], flux[mode_dev + m : mode_dev + m + 1]], 0)
        spots = mm_t(jnp.concatenate([-0.5 * flux] * halves, 1).astype(BF), wall_hot[...])
        blank = jnp.zeros((2 * mode_dev, nodes), F32)
        pulled = jnp.concatenate([blank, spots[:mode_dev], blank, spots[mode_dev:]], 0)

        field_sent(sec)
        for k in range(1, n_mode):
            arrive(e_own.at[sec, other_mode(k)], sec, s_eo + other_mode(k))
        here, back = gather_own(lanes(e_own, sec, n_mode))

        @pl.when(has_prev)
        def _():
            for j in range(n_mode):
                arrive(e_prev.at[sec, j], sec, s_ep + j)

        back = back + gather_prev(lanes(e_prev, sec, n_mode))

        @pl.when(has_next)
        def _():
            for j in range(ghosts):
                arrive(e_next.at[sec, j], sec, s_en + j)

        here = here + gather_next(lanes(e_next, sec, ghosts))
        curled = elements(here, back, 1)
        emf_sent(sec)
        total = scatter([x + y for x, y in zip(diffused, curled)]) + pulled
        return total * mass_inv - damp * value

    out_ref[...] = field_ref[...]

    def section(sec, carry):
        value = out_ref[...].reshape(rows, nodes)
        stage(sec, value)
        send_field(sec)
        stage_trace(sec)
        start(t_copies(sec))
        out_ref[...] = (value + 0.2 * rate(sec, value)).reshape(out_ref.shape)
        return carry

    lax.fori_loop(0, 2, section, 0)


def body(field, velocity, stiffness, curl_matrix, mass, connect, wall_index, dtn):
    n_mode = lax.axis_size("mode")
    n_mer = lax.axis_size("mer")
    mode_dev, _, nodes = field.shape
    modes = mode_dev * n_mode
    nphi = velocity.shape[1]
    elems, npe = connect.shape
    wall_dev = wall_index.shape[0]
    rows = mode_dev * 6
    chunk = nodes // n_mode
    ghosts = GHOST // chunk
    forward, inverse = transforms(modes, mode_dev, nphi)
    sems = 4 * n_mode + n_mer + 3
    vmem = pl.BlockSpec(memory_space=pltpu.VMEM)
    hbm = pl.BlockSpec(memory_space=pltpu.HBM)
    shapes = (
        jax.ShapeDtypeStruct((6, mode_dev, nodes), F32),
        jax.ShapeDtypeStruct((2, mode_dev, 2, wall_dev), F32),
    )
    turned = jnp.swapaxes(field, 0, 1)
    last, flux = pl.pallas_call(
        functools.partial(kernel, n_mode, n_mer, modes),
        out_shape=shapes,
        in_specs=[hbm] * 10,
        out_specs=(vmem, vmem),
        scratch_shapes=[
            pltpu.VMEM((2, rows, nodes), BF),
            pltpu.VMEM((2, n_mode, rows, chunk), BF),
            pltpu.VMEM((2, n_mode, rows, chunk), BF),
            pltpu.VMEM((2, rows, nodes), BF),
            pltpu.VMEM((2, rows, GHOST), BF),
            pltpu.VMEM((2, n_mode, rows, chunk), BF),
            pltpu.VMEM((2, n_mode, rows, chunk), BF),
            pltpu.VMEM((2, n_mode, rows, chunk), BF),
            pltpu.VMEM((2, ghosts, rows, chunk), BF),
            pltpu.VMEM((2, 2 * mode_dev, 128), BF),
            pltpu.VMEM((2, n_mer, 2 * mode_dev, 128), BF),
            pltpu.VMEM((elems, npe), jnp.int32),
            pltpu.VMEM((2, 256, 256), BF),
            pltpu.VMEM((2, nodes + GHOST, elems * npe), BF),
            pltpu.VMEM((nodes, 128), BF),
            pltpu.VMEM((6, mode_dev, nodes), F32),
            pltpu.VMEM(velocity.shape, BF),
            pltpu.VMEM(stiffness.shape, F32),
            pltpu.VMEM(curl_matrix.shape, F32),
            pltpu.VMEM((1, nodes), F32),
            pltpu.VMEM(connect.shape, jnp.int32),
            pltpu.VMEM((1, wall_dev), jnp.int32),
            pltpu.VMEM(dtn.shape, BF),
            pltpu.VMEM(forward.shape, F32),
            pltpu.VMEM(inverse.shape, F32),
            pltpu.SemaphoreType.DMA((2, sems)),
            pltpu.SemaphoreType.DMA((2, sems)),
            pltpu.SemaphoreType.DMA((10,)),
        ],
        compiler_params=pltpu.CompilerParams(
            collective_id=0, has_side_effects=True, vmem_limit_bytes=60 * 1024 * 1024
        ),
    )(
        turned,
        velocity,
        stiffness,
        curl_matrix,
        mass.reshape(1, nodes),
        connect,
        wall_index.reshape(1, wall_dev),
        dtn,
        forward,
        inverse,
    )
    advanced = 0.5 * (turned + last)
    return jnp.swapaxes(advanced, 0, 1), flux


def solution(mesh):
    placed = (
        P("mode", None, "mer"),
        P(None, None, ("mer", "mode")),
        P(),
        P(),
        P("mer"),
        P("mer", None),
        P("mer"),
        P("mode", "mer", None),
    )
    return jax.shard_map(
        body,
        mesh=mesh,
        in_specs=placed,
        out_specs=(P("mode", None, "mer"), P(None, "mode", None, "mer")),
        check_vma=False,
    )
```

```python
import functools

import jax
import jax.numpy as jnp
import numpy as np
from jax import lax
from jax.experimental import pallas as pl
from jax.experimental.pallas import tpu as pltpu
from jax.sharding import PartitionSpec as P

GHOST = 256
MESH = pl.DeviceIdType.MESH
BF = jnp.bfloat16
F32 = jnp.float32


def transforms(modes, mode_dev, nphi):
    angle = 2.0 * np.pi * ((np.arange(modes)[:, None] * np.arange(nphi)[None, :]) % nphi) / nphi
    table = np.stack([np.cos(angle), -np.sin(angle)], 1)
    forward = np.zeros((3, nphi, modes, 6))
    inverse = np.zeros((modes, 6, 3, nphi))
    for p in range(2):
        for c in range(3):
            forward[c, :, :, 3 * p + c] = table[:, p].T
            inverse[:, 3 * p + c, (c - 1) % 3, :] = table[:, p] / nphi
    owners = modes // mode_dev
    forward = forward.reshape(3 * nphi, owners, mode_dev, 6).transpose(0, 1, 3, 2).reshape(3 * nphi, modes * 6)
    inverse = inverse.reshape(owners, mode_dev, 6, 3 * nphi).transpose(0, 2, 1, 3).reshape(modes * 6, 3 * nphi)
    return jnp.asarray(forward, F32), jnp.asarray(inverse, F32)


def mm(a, b):
    return jnp.dot(a, b, preferred_element_type=F32)


def mm_t(a, b):
    return lax.dot_general(a, b, (((1,), (1,)), ((), ())), preferred_element_type=F32)


def onehot(hit):
    return jnp.where(hit, 1.0, 0.0).astype(BF)


def iota(shape, dim):
    return lax.broadcasted_iota(jnp.int32, shape, dim)


def kernel(
    n_mode,
    n_mer,
    modes,
    field_in,
    vel_in,
    stiff_in,
    curl_in,
    mass_in,
    connect_in,
    wall_in,
    dtn_in,
    forward_in,
    inverse_in,
    out_ref,
    flux_ref,
    f_full,
    f_part,
    f_got,
    f_prev,
    f_next,
    e_part,
    e_own,
    e_prev,
    e_next,
    t_part,
    t_got,
    c_prev,
    kmat,
    pick,
    wall_hot,
    field_ref,
    vel_ref,
    stiff_ref,
    curl_ref,
    mass_ref,
    connect_ref,
    wall_ref,
    dtn_ref,
    forward_ref,
    inverse_ref,
    send_sem,
    recv_sem,
    load_sem,
):
    _, mode_dev, nodes = field_ref.shape
    nphi = vel_ref.shape[1]
    rows = mode_dev * 6
    chunk = nodes // n_mode
    ghosts = GHOST // chunk
    elems, npe = connect_ref.shape
    wall_dev = wall_ref.shape[1]
    slots = elems * npe
    ext = nodes + GHOST
    me = lax.axis_index("mode")
    d = lax.axis_index("mer")
    has_prev = d > 0
    has_next = d < n_mer - 1

    def at(mode, mer):
        return {"mode": mode, "mer": mer}

    def other_mode(k):
        return lax.rem(me + k, n_mode)

    def other_mer(k):
        return lax.rem(d + k, n_mer)

    loads = [
        pltpu.make_async_copy(src, dst, load_sem.at[i])
        for i, (src, dst) in enumerate(
            [
                (field_in, field_ref),
                (connect_in, connect_ref),
                (wall_in, wall_ref),
                (stiff_in, stiff_ref),
                (curl_in, curl_ref),
                (forward_in, forward_ref),
                (vel_in, vel_ref),
                (inverse_in, inverse_ref),
                (dtn_in, dtn_ref),
                (mass_in, mass_ref),
            ]
        )
    ]
    loads[0].start()

    barrier = pltpu.get_barrier_semaphore()

    def greet(mode, mer):
        pl.semaphore_signal(barrier, inc=1, device_id=at(mode, mer), device_id_type=MESH)

    for k in range(1, n_mode):
        greet(other_mode(k), d)

    @pl.when(has_prev)
    def _():
        for k in range(n_mode):
            greet(other_mode(k), d - 1)

    @pl.when(has_next)
    def _():
        for k in range(n_mode):
            greet(other_mode(k), d + 1)

    for k in range(1, n_mer):
        peer = other_mer(k)

        @pl.when(jnp.logical_and(peer != d - 1, peer != d + 1))
        def _():
            greet(me, peer)

    for load in loads[1:]:
        load.start()

    s_f, s_eo, s_ep, s_en, s_fp, s_fn, s_t, s_c = range(8)

    def copy(src, dst, sec, no, mode, mer):
        return pltpu.make_async_remote_copy(
            src_ref=src,
            dst_ref=dst,
            send_sem=send_sem.at[sec, no],
            recv_sem=recv_sem.at[sec, no],
            device_id=at(mode, mer),
            device_id_type=MESH,
        )

    def f_copies(sec):
        return [
            copy(f_part.at[sec, other_mode(k)], f_got.at[sec, me], sec, s_f, other_mode(k), d)
            for k in range(1, n_mode)
        ]

    def t_copies(sec):
        return [
            copy(t_part.at[sec], t_got.at[sec, d], sec, s_t, me, other_mer(k))
            for k in range(1, n_mer)
        ]

    def up_copies(sec):
        made = [copy(f_full.at[sec], f_prev.at[sec], sec, s_fp, me, d + 1)]
        if sec == 0:
            made.append(copy(connect_ref, c_prev, sec, s_c, me, d + 1))
        return made

    def down_copies(sec):
        return [copy(f_full.at[sec, :, pl.ds(0, GHOST)], f_next.at[sec], sec, s_fn, me, d - 1)]

    def e_copies(sec):
        return [
            copy(e_part.at[sec, other_mode(k)], e_own.at[sec, me], sec, s_eo, other_mode(k), d)
            for k in range(1, n_mode)
        ]

    def e_up_copies(sec):
        return [
            copy(e_part.at[sec, other_mode(k)], e_prev.at[sec, me], sec, s_ep, other_mode(k), d + 1)
            for k in range(n_mode)
        ]

    def e_down_copies(sec):
        return [
            copy(e_part.at[sec, other_mode(k)], e_next.at[sec, me], sec, s_en, other_mode(k), d - 1)
            for k in range(n_mode)
        ]

    sends_down = jnp.logical_and(has_prev, me < ghosts)

    def start(copies):
        for c in copies:
            c.start()

    def sent(ref, sec, no):
        copy(ref, ref, sec, no, me, d).wait_send()

    def arrive(ref, sec, no):
        copy(ref, ref, sec, no, me, d).wait_recv()

    most = pl.ds(0, n_mode - 1)
    others = pl.ds(0, n_mer - 1)

    halves = 128 // wall_dev

    def stage(sec, value):
        low = value.astype(BF)
        f_full[sec] = low
        for j in range(n_mode):
            f_part[sec, j] = low[:, j * chunk : (j + 1) * chunk]
        f_got[sec, me] = f_part[sec, me]

    def stage_trace(sec):
        low = f_full[sec]
        picked = jnp.concatenate([low[r * mode_dev : (r + 1) * mode_dev] for r in (2, 5)], 0)
        walls = mm(picked, wall_hot[...]).astype(BF)
        t_part[sec] = walls
        t_got[sec, d] = walls

    def send_field(sec):
        start(f_copies(sec))

        @pl.when(has_next)
        def _():
            start(up_copies(sec))

        @pl.when(has_prev)
        def _():
            start(down_copies(sec))

    loads[0].wait()
    field = field_ref[...].reshape(rows, nodes)
    stage(0, field)

    @pl.when(jnp.logical_not(has_prev))
    def _():
        f_prev[...] = jnp.zeros(f_prev.shape, BF)
        e_prev[...] = jnp.zeros(e_prev.shape, BF)
        c_prev[...] = jnp.full(c_prev.shape, -1, jnp.int32)

    @pl.when(jnp.logical_not(has_next))
    def _():
        f_next[...] = jnp.zeros(f_next.shape, BF)
        e_next[...] = jnp.zeros(e_next.shape, BF)

    prev_n = has_prev.astype(jnp.int32)
    next_n = has_next.astype(jnp.int32)
    pl.semaphore_wait(barrier, n_mode - 1 + n_mer - 1 + (n_mode - 1) * (prev_n + next_n))

    loads[1].wait()
    send_field(0)

    step = 128

    def fill_pick(which, ref):
        numbers = jnp.concatenate([ref[e : e + 1, :] for e in range(elems)], 1)

        def fill(i, carry):
            base = pl.multiple_of(i * step, step)
            pick[which, pl.ds(base, step), :] = onehot(iota((step, slots), 0) + base == numbers)
            return carry

        lax.fori_loop(0, ext // step, fill, 0)

    loads[2].wait()
    wall_row = jnp.concatenate([wall_ref[...]] * halves, 1)
    lane = iota((1, 128), 1)
    wall_row = jnp.where(lane // wall_dev == lax.rem(d, halves), wall_row, -1)
    wall_hot[...] = onehot(iota((nodes, 128), 0) == wall_row)
    stage_trace(0)
    start(t_copies(0))

    wide_dim = 256
    group = wide_dim // npe
    groups = slots // wide_dim
    same = iota((wide_dim, wide_dim), 0) // npe == iota((wide_dim, wide_dim), 1) // npe

    def spread(ref, sign):
        turned = jnp.concatenate([sign * ref[...].T] * group, 1)
        return jnp.where(same, jnp.concatenate([turned] * group, 0), 0.0).astype(BF)

    def prepare():
        fill_pick(0, connect_ref)
        loads[3].wait()
        kmat[0] = spread(stiff_ref, -1.0)
        loads[4].wait()
        kmat[1] = spread(curl_ref, 1.0)

        @pl.when(has_prev)
        def _():
            arrive(c_prev, 0, s_c)

        fill_pick(1, c_prev)

    for load in loads[5:8] + loads[9:]:
        load.wait()
    mass_inv = 1.0 / mass_ref[...]
    mode_no = me * mode_dev + lax.rem(iota((rows, 1), 0), mode_dev)
    damp = 4.0 * (mode_no.astype(F32) / modes) ** 2

    def elements(here, back, which):
        low = (here.astype(BF), back.astype(BF))
        tall = jnp.concatenate([x[:, g * wide_dim : (g + 1) * wide_dim] for x in low for g in range(groups)], 0)
        done = mm(tall, kmat[which])
        return [done[i * rows : (i + 1) * rows] for i in range(2 * groups)]

    def gather_own(own):
        return mm(own, pick[0, :nodes, :]), mm(own[:, :GHOST], pick[1, nodes:, :])

    def gather_next(nxt):
        return mm(nxt, pick[0, nodes:, :])

    def gather_prev(prv):
        return mm(prv, pick[1, :nodes, :])

    def scatter(parts):
        low = [x.astype(BF) for x in parts]
        total = mm_t(pick[0, :nodes, :], jnp.concatenate(low[:groups], 1))
        extra = mm_t(pick[1, nodes:, :], jnp.concatenate(low[groups:], 1))
        return jnp.concatenate([total[:GHOST] + extra, total[GHOST:]], 0).T

    def lanes(ref, sec, count):
        return jnp.concatenate([ref[sec, j] for j in range(count)], 1)

    def all_sent(sec):
        sent(f_part.at[sec, most], sec, s_f)
        sent(t_got.at[sec, others], sec, s_t)
        sent(e_part.at[sec, most], sec, s_eo)

        @pl.when(has_next)
        def _():
            sent(f_full.at[sec], sec, s_fp)
            if sec == 0:
                sent(connect_ref, sec, s_c)
            sent(e_part.at[sec], sec, s_ep)

        @pl.when(has_prev)
        def _():
            sent(f_next.at[sec], sec, s_fn)

        @pl.when(sends_down)
        def _():
            sent(e_part.at[sec], sec, s_en)

    def rate(sec, value):
        arrive(f_got.at[sec, most], sec, s_f)
        phys = mm(forward_ref[...].astype(BF), f_got[sec].reshape(n_mode * rows, chunk))
        px, py, pz = [phys[c * nphi : (c + 1) * nphi] for c in range(3)]
        vx, vy, vz = [vel_ref[c].astype(F32) for c in range(3)]
        cross = jnp.concatenate([vy * pz - vz * py, vz * px - vx * pz, vx * py - vy * px], 0)
        emf = mm(inverse_ref[...].astype(BF), cross.astype(BF)).astype(BF)
        e_part[sec] = emf.reshape(n_mode, rows, chunk)
        e_own[sec, me] = e_part[sec, me]
        start(e_copies(sec))

        @pl.when(has_next)
        def _():
            start(e_up_copies(sec))

        @pl.when(sends_down)
        def _():
            start(e_down_copies(sec))

        if sec == 0:
            prepare()
            loads[8].wait()
        else:
            all_sent(0)

        @pl.when(has_prev)
        def _():
            arrive(f_prev.at[sec], sec, s_fp)

        @pl.when(has_next)
        def _():
            arrive(f_next.at[sec], sec, s_fn)

        here, back = gather_own(f_full[sec])
        diffused = elements(here + gather_next(f_next[sec]), back + gather_prev(f_prev[sec]), 0)

        arrive(t_got.at[sec, others], sec, s_t)
        trace = jnp.concatenate(
            [sum([t_got[sec, i + h] for h in range(1, halves)], t_got[sec, i]) for i in range(0, n_mer, halves)], 1
        )
        wide = mm_t(dtn_ref[...].reshape(mode_dev * wall_dev, trace.shape[1]), trace).T
        wide = jnp.where(iota(wide.shape, 1) // wall_dev == lax.rem(iota(wide.shape, 0), mode_dev), wide, 0.0)
        folded = sum([wide[:, i : i + 128] for i in range(128, wide.shape[1], 128)], wide[:, :128])
        flux = sum([folded[:, h * wall_dev : (h + 1) * wall_dev] for h in range(1, halves)], folded[:, :wall_dev])
        for m in range(mode_dev):
            flux_ref[sec, m] = jnp.concatenate([flux[m : m + 1], flux[mode_dev + m : mode_dev + m + 1]], 0)
        spots = mm_t(wall_hot[...], jnp.concatenate([-0.5 * flux] * halves, 1).astype(BF)).T
        blank = jnp.zeros((2 * mode_dev, nodes), F32)
        pulled = jnp.concatenate([blank, spots[:mode_dev], blank, spots[mode_dev:]], 0)

        arrive(e_own.at[sec, most], sec, s_eo)
        here, back = gather_own(lanes(e_own, sec, n_mode))

        @pl.when(has_prev)
        def _():
            arrive(e_prev.at[sec], sec, s_ep)

        back = back + gather_prev(lanes(e_prev, sec, n_mode))

        @pl.when(has_next)
        def _():
            arrive(e_next.at[sec], sec, s_en)

        here = here + gather_next(lanes(e_next, sec, ghosts))
        curled = elements(here, back, 1)
        total = scatter([x + y for x, y in zip(diffused, curled)]) + pulled
        return total * mass_inv - damp * value

    section = field + 0.2 * rate(0, field)
    stage(1, section)
    send_field(1)
    stage_trace(1)
    start(t_copies(1))
    second = rate(1, section)
    advanced = 0.5 * (field + section + 0.2 * second)
    out_ref[...] = advanced.reshape(out_ref.shape)

    all_sent(1)


def finish(out_in, flux_in, out_ref, flux_ref, out_mid, flux_mid, sem):
    routes = [(flux_in, flux_mid, flux_ref), (out_in, out_mid, out_ref)]
    inward = [pltpu.make_async_copy(a, b, sem.at[i]) for i, (a, b, _) in enumerate(routes)]
    outward = [pltpu.make_async_copy(b, c, sem.at[2 + i]) for i, (_, b, c) in enumerate(routes)]
    for c in inward:
        c.start()
    for c, then in zip(inward, outward):
        c.wait()
        then.start()
    for c in outward:
        c.wait()


def body(field, velocity, stiffness, curl_matrix, mass, connect, wall_index, dtn):
    n_mode = lax.axis_size("mode")
    n_mer = lax.axis_size("mer")
    mode_dev, _, nodes = field.shape
    modes = mode_dev * n_mode
    nphi = velocity.shape[1]
    elems, npe = connect.shape
    wall_dev = wall_index.shape[0]
    rows = mode_dev * 6
    chunk = nodes // n_mode
    ghosts = GHOST // chunk
    forward, inverse = transforms(modes, mode_dev, nphi)
    vmem = pl.BlockSpec(memory_space=pltpu.VMEM)
    hbm = pl.BlockSpec(memory_space=pltpu.HBM)
    shapes = (
        jax.ShapeDtypeStruct((6, mode_dev, nodes), F32),
        jax.ShapeDtypeStruct((2, mode_dev, 2, wall_dev), F32),
    )
    advanced, flux = pl.pallas_call(
        functools.partial(kernel, n_mode, n_mer, modes),
        out_shape=shapes,
        in_specs=[hbm] * 10,
        out_specs=(vmem, vmem),
        scratch_shapes=[
            pltpu.VMEM((2, rows, nodes), BF),
            pltpu.VMEM((2, n_mode, rows, chunk), BF),
            pltpu.VMEM((2, n_mode, rows, chunk), BF),
            pltpu.VMEM((2, rows, nodes), BF),
            pltpu.VMEM((2, rows, GHOST), BF),
            pltpu.VMEM((2, n_mode, rows, chunk), BF),
            pltpu.VMEM((2, n_mode, rows, chunk), BF),
            pltpu.VMEM((2, n_mode, rows, chunk), BF),
            pltpu.VMEM((2, ghosts, rows, chunk), BF),
            pltpu.VMEM((2, 2 * mode_dev, 128), BF),
            pltpu.VMEM((2, n_mer, 2 * mode_dev, 128), BF),
            pltpu.VMEM((elems, npe), jnp.int32),
            pltpu.VMEM((2, 256, 256), BF),
            pltpu.VMEM((2, nodes + GHOST, elems * npe), BF),
            pltpu.VMEM((nodes, 128), BF),
            pltpu.VMEM((6, mode_dev, nodes), F32),
            pltpu.VMEM(velocity.shape, BF),
            pltpu.VMEM(stiffness.shape, F32),
            pltpu.VMEM(curl_matrix.shape, F32),
            pltpu.VMEM((1, nodes), F32),
            pltpu.VMEM(connect.shape, jnp.int32),
            pltpu.VMEM((1, wall_dev), jnp.int32),
            pltpu.VMEM(dtn.shape, BF),
            pltpu.VMEM(forward.shape, F32),
            pltpu.VMEM(inverse.shape, F32),
            pltpu.SemaphoreType.DMA((2, 8)),
            pltpu.SemaphoreType.DMA((2, 8)),
            pltpu.SemaphoreType.DMA((10,)),
        ],
        compiler_params=pltpu.CompilerParams(
            collective_id=0, has_side_effects=True, vmem_limit_bytes=60 * 1024 * 1024
        ),
    )(
        jnp.swapaxes(field, 0, 1),
        velocity,
        stiffness,
        curl_matrix,
        mass.reshape(1, nodes),
        connect,
        wall_index.reshape(1, wall_dev),
        dtn,
        forward,
        inverse,
    )
    advanced, flux = pl.pallas_call(
        finish,
        out_shape=shapes,
        in_specs=[hbm] * 2,
        out_specs=(hbm, hbm),
        scratch_shapes=[
            pltpu.VMEM(shapes[0].shape, F32),
            pltpu.VMEM(shapes[1].shape, F32),
            pltpu.SemaphoreType.DMA((4,)),
        ],
        compiler_params=pltpu.CompilerParams(vmem_limit_bytes=60 * 1024 * 1024),
    )(advanced, flux)
    return jnp.swapaxes(advanced, 0, 1), flux


def solution(mesh):
    placed = (
        P("mode", None, "mer"),
        P(None, None, ("mer", "mode")),
        P(),
        P(),
        P("mer"),
        P("mer", None),
        P("mer"),
        P("mode", "mer", None),
    )
    return jax.shard_map(
        body,
        mesh=mesh,
        in_specs=placed,
        out_specs=(P("mode", None, "mer"), P(None, "mode", None, "mer")),
        check_vma=False,
    )
```

```python
import functools

import jax
import jax.numpy as jnp
import numpy as np
from jax import lax
from jax.experimental import pallas as pl
from jax.experimental.pallas import tpu as pltpu
from jax.sharding import PartitionSpec as P

GHOST = 256
MESH = pl.DeviceIdType.MESH
BF = jnp.bfloat16
F32 = jnp.float32


def transforms(modes, mode_dev, nphi):
    angle = 2.0 * np.pi * ((np.arange(modes)[:, None] * np.arange(nphi)[None, :]) % nphi) / nphi
    table = np.stack([np.cos(angle), -np.sin(angle)], 1)
    forward = np.zeros((3, nphi, modes, 6))
    inverse = np.zeros((modes, 6, 3, nphi))
    for p in range(2):
        for c in range(3):
            forward[c, :, :, 3 * p + c] = table[:, p].T
            inverse[:, 3 * p + c, (c - 1) % 3, :] = table[:, p] / nphi
    owners = modes // mode_dev
    forward = forward.reshape(3 * nphi, owners, mode_dev, 6).transpose(0, 1, 3, 2).reshape(3 * nphi, modes * 6)
    inverse = inverse.reshape(owners, mode_dev, 6, 3 * nphi).transpose(0, 2, 1, 3).reshape(modes * 6, 3 * nphi)
    return jnp.asarray(forward, F32), jnp.asarray(inverse, F32)


def mm(a, b):
    return jnp.dot(a, b, preferred_element_type=F32)


def mm_t(a, b):
    return lax.dot_general(a, b, (((1,), (1,)), ((), ())), preferred_element_type=F32)


def onehot(hit):
    return jnp.where(hit, 1.0, 0.0).astype(BF)


def iota(shape, dim):
    return lax.broadcasted_iota(jnp.int32, shape, dim)


def kernel(
    n_mode,
    n_mer,
    modes,
    field_in,
    vel_in,
    stiff_in,
    curl_in,
    mass_in,
    connect_in,
    wall_in,
    dtn_in,
    forward_in,
    inverse_in,
    out_ref,
    flux_ref,
    f_full,
    f_part,
    f_got,
    f_prev,
    f_next,
    e_part,
    e_own,
    e_prev,
    e_next,
    t_part,
    t_got,
    c_prev,
    kmat,
    pick,
    wall_hot,
    field_ref,
    vel_ref,
    stiff_ref,
    curl_ref,
    mass_ref,
    connect_ref,
    wall_ref,
    dtn_ref,
    forward_ref,
    inverse_ref,
    send_sem,
    recv_sem,
    load_sem,
):
    _, mode_dev, nodes = field_ref.shape
    nphi = vel_ref.shape[1]
    rows = mode_dev * 6
    chunk = nodes // n_mode
    ghosts = GHOST // chunk
    elems, npe = connect_ref.shape
    wall_dev = wall_ref.shape[1]
    slots = elems * npe
    ext = nodes + GHOST
    me = lax.axis_index("mode")
    d = lax.axis_index("mer")
    has_prev = d > 0
    has_next = d < n_mer - 1

    def at(mode, mer):
        return {"mode": mode, "mer": mer}

    def other_mode(k):
        return lax.rem(me + k, n_mode)

    def other_mer(k):
        return lax.rem(d + k, n_mer)

    loads = [
        pltpu.make_async_copy(src, dst, load_sem.at[i])
        for i, (src, dst) in enumerate(
            [
                (field_in, field_ref),
                (connect_in, connect_ref),
                (wall_in, wall_ref),
                (stiff_in, stiff_ref),
                (curl_in, curl_ref),
                (forward_in, forward_ref),
                (vel_in, vel_ref),
                (inverse_in, inverse_ref),
                (dtn_in, dtn_ref),
                (mass_in, mass_ref),
            ]
        )
    ]
    loads[0].start()

    barrier = pltpu.get_barrier_semaphore()

    def greet(mode, mer):
        pl.semaphore_signal(barrier, inc=1, device_id=at(mode, mer), device_id_type=MESH)

    for k in range(1, n_mode):
        greet(other_mode(k), d)

    for k in range(1, n_mer):
        greet(me, other_mer(k))

    for load in loads[1:]:
        load.start()

    s_f, s_eo, s_ep, s_en, s_fp, s_fn, s_t, s_c = range(8)

    def copy(src, dst, sec, no, mode, mer):
        return pltpu.make_async_remote_copy(
            src_ref=src,
            dst_ref=dst,
            send_sem=send_sem.at[sec, no],
            recv_sem=recv_sem.at[sec, no],
            device_id=at(mode, mer),
            device_id_type=MESH,
        )

    def f_copies(sec):
        return [
            copy(f_part.at[sec, other_mode(k)], f_got.at[sec, me], sec, s_f, other_mode(k), d)
            for k in range(1, n_mode)
        ]

    def t_copies(sec):
        return [
            copy(t_part.at[sec], t_got.at[sec, d], sec, s_t, me, other_mer(k))
            for k in range(1, n_mer)
        ]

    def up_copies(sec):
        made = [copy(f_full.at[sec], f_prev.at[sec], sec, s_fp, me, d + 1)]
        if sec == 0:
            made.append(copy(connect_ref, c_prev, sec, s_c, me, d + 1))
        return made

    def down_copies(sec):
        return [copy(f_full.at[sec, :, pl.ds(0, GHOST)], f_next.at[sec], sec, s_fn, me, d - 1)]

    def e_copies(sec):
        return [
            copy(e_part.at[sec, other_mode(k)], e_own.at[sec, me], sec, s_eo, other_mode(k), d)
            for k in range(1, n_mode)
        ]

    def e_up_copies(sec):
        return [copy(e_own.at[sec], e_prev.at[sec], sec, s_ep, me, d + 1)]

    def e_down_copies(sec):
        return [copy(e_own.at[sec, pl.ds(0, ghosts)], e_next.at[sec], sec, s_en, me, d - 1)]

    def start(copies):
        for c in copies:
            c.start()

    def sent(ref, sec, no):
        copy(ref, ref, sec, no, me, d).wait_send()

    def arrive(ref, sec, no):
        copy(ref, ref, sec, no, me, d).wait_recv()

    most = pl.ds(0, n_mode - 1)
    others = pl.ds(0, n_mer - 1)

    halves = 128 // wall_dev

    def stage(sec, value):
        low = value.astype(BF)
        f_full[sec] = low
        for j in range(n_mode):
            f_part[sec, j] = low[:, j * chunk : (j + 1) * chunk]
        f_got[sec, me] = f_part[sec, me]

    def stage_trace(sec):
        low = f_full[sec]
        picked = jnp.concatenate([low[r * mode_dev : (r + 1) * mode_dev] for r in (2, 5)], 0)
        walls = mm(picked, wall_hot[...]).astype(BF)
        t_part[sec] = walls
        t_got[sec, d] = walls

    def send_field(sec):
        start(f_copies(sec))

        @pl.when(has_next)
        def _():
            start(up_copies(sec))

        @pl.when(has_prev)
        def _():
            start(down_copies(sec))

    loads[0].wait()
    field = field_ref[...].reshape(rows, nodes)
    stage(0, field)

    @pl.when(jnp.logical_not(has_prev))
    def _():
        f_prev[...] = jnp.zeros(f_prev.shape, BF)
        e_prev[...] = jnp.zeros(e_prev.shape, BF)
        c_prev[...] = jnp.full(c_prev.shape, -1, jnp.int32)

    @pl.when(jnp.logical_not(has_next))
    def _():
        f_next[...] = jnp.zeros(f_next.shape, BF)
        e_next[...] = jnp.zeros(e_next.shape, BF)

    pl.semaphore_wait(barrier, n_mode - 1 + n_mer - 1)

    loads[1].wait()
    send_field(0)

    step = 128

    def fill_pick(which, ref):
        numbers = jnp.concatenate([ref[e : e + 1, :] for e in range(elems)], 1)

        def fill(i, carry):
            base = pl.multiple_of(i * step, step)
            pick[which, pl.ds(base, step), :] = onehot(iota((step, slots), 0) + base == numbers)
            return carry

        lax.fori_loop(0, ext // step, fill, 0)

    loads[2].wait()
    wall_row = jnp.concatenate([wall_ref[...]] * halves, 1)
    lane = iota((1, 128), 1)
    wall_row = jnp.where(lane // wall_dev == lax.rem(d, halves), wall_row, -1)
    wall_hot[...] = onehot(iota((nodes, 128), 0) == wall_row)
    stage_trace(0)
    start(t_copies(0))

    wide_dim = 256
    group = wide_dim // npe
    groups = slots // wide_dim
    same = iota((wide_dim, wide_dim), 0) // npe == iota((wide_dim, wide_dim), 1) // npe

    def spread(ref, sign):
        turned = jnp.concatenate([sign * ref[...].T] * group, 1)
        return jnp.where(same, jnp.concatenate([turned] * group, 0), 0.0).astype(BF)

    def prepare():
        fill_pick(0, connect_ref)
        loads[3].wait()
        kmat[0] = spread(stiff_ref, -1.0)
        loads[4].wait()
        kmat[1] = spread(curl_ref, 1.0)

        @pl.when(has_prev)
        def _():
            arrive(c_prev, 0, s_c)

        fill_pick(1, c_prev)

    for load in loads[5:8] + loads[9:]:
        load.wait()
    mass_inv = 1.0 / mass_ref[...]
    mode_no = me * mode_dev + lax.rem(iota((rows, 1), 0), mode_dev)
    damp = 4.0 * (mode_no.astype(F32) / modes) ** 2

    def elements(here, back, which):
        low = (here.astype(BF), back.astype(BF))
        tall = jnp.concatenate([x[:, g * wide_dim : (g + 1) * wide_dim] for x in low for g in range(groups)], 0)
        done = mm(tall, kmat[which])
        return [done[i * rows : (i + 1) * rows] for i in range(2 * groups)]

    def gather_own(own):
        return mm(own, pick[0, :nodes, :]), mm(own[:, :GHOST], pick[1, nodes:, :])

    def gather_next(nxt):
        return mm(nxt, pick[0, nodes:, :])

    def gather_prev(prv):
        return mm(prv, pick[1, :nodes, :])

    def scatter(parts):
        low = [x.astype(BF) for x in parts]
        total = mm_t(jnp.concatenate(low[:groups], 1), pick[0, :nodes, :])
        extra = mm_t(jnp.concatenate(low[groups:], 1), pick[1, nodes:, :])
        return jnp.concatenate([total[:, :GHOST] + extra, total[:, GHOST:]], 1)

    def lanes(ref, sec, count):
        return jnp.concatenate([ref[sec, j] for j in range(count)], 1)

    def all_sent(sec):
        sent(f_part.at[sec, most], sec, s_f)
        sent(t_got.at[sec, others], sec, s_t)
        sent(e_part.at[sec, most], sec, s_eo)

        @pl.when(has_next)
        def _():
            sent(f_full.at[sec], sec, s_fp)
            if sec == 0:
                sent(connect_ref, sec, s_c)
            sent(e_own.at[sec], sec, s_ep)

        @pl.when(has_prev)
        def _():
            sent(f_next.at[sec], sec, s_fn)
            sent(e_next.at[sec], sec, s_en)

    def rate(sec, value):
        arrive(f_got.at[sec, most], sec, s_f)
        phys = mm(forward_ref[...].astype(BF), f_got[sec].reshape(n_mode * rows, chunk))
        px, py, pz = [phys[c * nphi : (c + 1) * nphi] for c in range(3)]
        vx, vy, vz = [vel_ref[c].astype(F32) for c in range(3)]
        cross = jnp.concatenate([vy * pz - vz * py, vz * px - vx * pz, vx * py - vy * px], 0)
        emf = mm(inverse_ref[...].astype(BF), cross.astype(BF)).astype(BF)
        e_part[sec] = emf.reshape(n_mode, rows, chunk)
        e_own[sec, me] = e_part[sec, me]
        start(e_copies(sec))

        if sec == 0:
            prepare()
            loads[8].wait()
        else:
            all_sent(0)

        @pl.when(has_prev)
        def _():
            arrive(f_prev.at[sec], sec, s_fp)

        @pl.when(has_next)
        def _():
            arrive(f_next.at[sec], sec, s_fn)

        here, back = gather_own(f_full[sec])
        diffused = elements(here + gather_next(f_next[sec]), back + gather_prev(f_prev[sec]), 0)

        arrive(t_got.at[sec, others], sec, s_t)
        trace = jnp.concatenate(
            [sum([t_got[sec, i + h] for h in range(1, halves)], t_got[sec, i]) for i in range(0, n_mer, halves)], 1
        )
        wide = mm_t(trace, dtn_ref[...].reshape(mode_dev * wall_dev, trace.shape[1]))
        wide = jnp.where(iota(wide.shape, 1) // wall_dev == lax.rem(iota(wide.shape, 0), mode_dev), wide, 0.0)
        folded = sum([wide[:, i : i + 128] for i in range(128, wide.shape[1], 128)], wide[:, :128])
        flux = sum([folded[:, h * wall_dev : (h + 1) * wall_dev] for h in range(1, halves)], folded[:, :wall_dev])
        for m in range(mode_dev):
            flux_ref[sec, m] = jnp.concatenate([flux[m : m + 1], flux[mode_dev + m : mode_dev + m + 1]], 0)
        spots = mm_t(jnp.concatenate([-0.5 * flux] * halves, 1).astype(BF), wall_hot[...])
        blank = jnp.zeros((2 * mode_dev, nodes), F32)
        pulled = jnp.concatenate([blank, spots[:mode_dev], blank, spots[mode_dev:]], 0)

        arrive(e_own.at[sec, most], sec, s_eo)

        @pl.when(has_next)
        def _():
            start(e_up_copies(sec))

        @pl.when(has_prev)
        def _():
            start(e_down_copies(sec))

        here, back = gather_own(lanes(e_own, sec, n_mode))

        @pl.when(has_prev)
        def _():
            arrive(e_prev.at[sec], sec, s_ep)

        back = back + gather_prev(lanes(e_prev, sec, n_mode))

        @pl.when(has_next)
        def _():
            arrive(e_next.at[sec], sec, s_en)

        here = here + gather_next(lanes(e_next, sec, ghosts))
        curled = elements(here, back, 1)
        total = scatter([x + y for x, y in zip(diffused, curled)]) + pulled
        return total * mass_inv - damp * value

    section = field + 0.2 * rate(0, field)
    stage(1, section)
    send_field(1)
    stage_trace(1)
    start(t_copies(1))
    second = rate(1, section)
    advanced = 0.5 * (field + section + 0.2 * second)
    out_ref[...] = advanced.reshape(out_ref.shape)

    all_sent(1)


def finish(out_in, flux_in, out_ref, flux_ref, out_mid, flux_mid, sem):
    routes = [(flux_in, flux_mid, flux_ref), (out_in, out_mid, out_ref)]
    inward = [pltpu.make_async_copy(a, b, sem.at[i]) for i, (a, b, _) in enumerate(routes)]
    outward = [pltpu.make_async_copy(b, c, sem.at[2 + i]) for i, (_, b, c) in enumerate(routes)]
    for c in inward:
        c.start()
    for c, then in zip(inward, outward):
        c.wait()
        then.start()
    for c in outward:
        c.wait()


def body(field, velocity, stiffness, curl_matrix, mass, connect, wall_index, dtn):
    n_mode = lax.axis_size("mode")
    n_mer = lax.axis_size("mer")
    mode_dev, _, nodes = field.shape
    modes = mode_dev * n_mode
    nphi = velocity.shape[1]
    elems, npe = connect.shape
    wall_dev = wall_index.shape[0]
    rows = mode_dev * 6
    chunk = nodes // n_mode
    ghosts = GHOST // chunk
    forward, inverse = transforms(modes, mode_dev, nphi)
    vmem = pl.BlockSpec(memory_space=pltpu.VMEM)
    hbm = pl.BlockSpec(memory_space=pltpu.HBM)
    shapes = (
        jax.ShapeDtypeStruct((6, mode_dev, nodes), F32),
        jax.ShapeDtypeStruct((2, mode_dev, 2, wall_dev), F32),
    )
    advanced, flux = pl.pallas_call(
        functools.partial(kernel, n_mode, n_mer, modes),
        out_shape=shapes,
        in_specs=[hbm] * 10,
        out_specs=(vmem, vmem),
        scratch_shapes=[
            pltpu.VMEM((2, rows, nodes), BF),
            pltpu.VMEM((2, n_mode, rows, chunk), BF),
            pltpu.VMEM((2, n_mode, rows, chunk), BF),
            pltpu.VMEM((2, rows, nodes), BF),
            pltpu.VMEM((2, rows, GHOST), BF),
            pltpu.VMEM((2, n_mode, rows, chunk), BF),
            pltpu.VMEM((2, n_mode, rows, chunk), BF),
            pltpu.VMEM((2, n_mode, rows, chunk), BF),
            pltpu.VMEM((2, ghosts, rows, chunk), BF),
            pltpu.VMEM((2, 2 * mode_dev, 128), BF),
            pltpu.VMEM((2, n_mer, 2 * mode_dev, 128), BF),
            pltpu.VMEM((elems, npe), jnp.int32),
            pltpu.VMEM((2, 256, 256), BF),
            pltpu.VMEM((2, nodes + GHOST, elems * npe), BF),
            pltpu.VMEM((nodes, 128), BF),
            pltpu.VMEM((6, mode_dev, nodes), F32),
            pltpu.VMEM(velocity.shape, BF),
            pltpu.VMEM(stiffness.shape, F32),
            pltpu.VMEM(curl_matrix.shape, F32),
            pltpu.VMEM((1, nodes), F32),
            pltpu.VMEM(connect.shape, jnp.int32),
            pltpu.VMEM((1, wall_dev), jnp.int32),
            pltpu.VMEM(dtn.shape, BF),
            pltpu.VMEM(forward.shape, F32),
            pltpu.VMEM(inverse.shape, F32),
            pltpu.SemaphoreType.DMA((2, 8)),
            pltpu.SemaphoreType.DMA((2, 8)),
            pltpu.SemaphoreType.DMA((10,)),
        ],
        compiler_params=pltpu.CompilerParams(
            collective_id=0, has_side_effects=True, vmem_limit_bytes=60 * 1024 * 1024
        ),
    )(
        jnp.swapaxes(field, 0, 1),
        velocity,
        stiffness,
        curl_matrix,
        mass.reshape(1, nodes),
        connect,
        wall_index.reshape(1, wall_dev),
        dtn,
        forward,
        inverse,
    )
    advanced, flux = pl.pallas_call(
        finish,
        out_shape=shapes,
        in_specs=[hbm] * 2,
        out_specs=(hbm, hbm),
        scratch_shapes=[
            pltpu.VMEM(shapes[0].shape, F32),
            pltpu.VMEM(shapes[1].shape, F32),
            pltpu.SemaphoreType.DMA((4,)),
        ],
        compiler_params=pltpu.CompilerParams(vmem_limit_bytes=60 * 1024 * 1024),
    )(advanced, flux)
    return jnp.swapaxes(advanced, 0, 1), flux


def solution(mesh):
    placed = (
        P("mode", None, "mer"),
        P(None, None, ("mer", "mode")),
        P(),
        P(),
        P("mer"),
        P("mer", None),
        P("mer"),
        P("mode", "mer", None),
    )
    return jax.shard_map(
        body,
        mesh=mesh,
        in_specs=placed,
        out_specs=(P("mode", None, "mer"), P(None, "mode", None, "mer")),
        check_vma=False,
    )
```

```python
import functools

import jax
import jax.numpy as jnp
import numpy as np
from jax import lax
from jax.experimental import pallas as pl
from jax.experimental.pallas import tpu as pltpu
from jax.sharding import PartitionSpec as P

GHOST = 256
MESH = pl.DeviceIdType.MESH
BF = jnp.bfloat16
F32 = jnp.float32


def transforms(modes, mode_dev, nphi):
    angle = 2.0 * np.pi * ((np.arange(modes)[:, None] * np.arange(nphi)[None, :]) % nphi) / nphi
    table = np.stack([np.cos(angle), -np.sin(angle)], 1)
    forward = np.zeros((3, nphi, modes, 6))
    inverse = np.zeros((modes, 6, 3, nphi))
    for p in range(2):
        for c in range(3):
            forward[c, :, :, 3 * p + c] = table[:, p].T
            inverse[:, 3 * p + c, (c - 1) % 3, :] = table[:, p] / nphi
    owners = modes // mode_dev
    forward = forward.reshape(3 * nphi, owners, mode_dev, 6).transpose(0, 1, 3, 2).reshape(3 * nphi, modes * 6)
    inverse = inverse.reshape(owners, mode_dev, 6, 3 * nphi).transpose(0, 2, 1, 3).reshape(modes * 6, 3 * nphi)
    return jnp.asarray(forward, F32), jnp.asarray(inverse, F32)


def mm(a, b):
    return jnp.dot(a, b, preferred_element_type=F32)


def mm_t(a, b):
    return lax.dot_general(a, b, (((1,), (1,)), ((), ())), preferred_element_type=F32)


def onehot(hit):
    return jnp.where(hit, 1.0, 0.0).astype(BF)


def iota(shape, dim):
    return lax.broadcasted_iota(jnp.int32, shape, dim)


def kernel(
    n_mode,
    n_mer,
    modes,
    field_in,
    vel_in,
    stiff_in,
    curl_in,
    mass_in,
    connect_in,
    wall_in,
    dtn_in,
    forward_in,
    inverse_in,
    out_ref,
    flux_ref,
    f_full,
    f_part,
    f_got,
    f_prev,
    f_next,
    e_part,
    e_own,
    e_prev,
    e_next,
    t_part,
    t_got,
    c_prev,
    kmat,
    pick,
    wall_hot,
    field_ref,
    vel_ref,
    stiff_ref,
    curl_ref,
    mass_ref,
    connect_ref,
    wall_ref,
    dtn_ref,
    forward_ref,
    inverse_ref,
    send_sem,
    recv_sem,
    load_sem,
):
    _, mode_dev, nodes = field_ref.shape
    nphi = vel_ref.shape[1]
    rows = mode_dev * 6
    chunk = nodes // n_mode
    ghosts = GHOST // chunk
    elems, npe = connect_ref.shape
    wall_dev = wall_ref.shape[1]
    slots = elems * npe
    ext = nodes + GHOST
    me = lax.axis_index("mode")
    d = lax.axis_index("mer")
    has_prev = d > 0
    has_next = d < n_mer - 1

    def at(mode, mer):
        return {"mode": mode, "mer": mer}

    def other_mode(k):
        return lax.rem(me + k, n_mode)

    def other_mer(k):
        return lax.rem(d + k, n_mer)

    loads = [
        pltpu.make_async_copy(src, dst, load_sem.at[i])
        for i, (src, dst) in enumerate(
            [
                (field_in, field_ref),
                (connect_in, connect_ref),
                (wall_in, wall_ref),
                (stiff_in, stiff_ref),
                (curl_in, curl_ref),
                (forward_in, forward_ref),
                (vel_in, vel_ref),
                (inverse_in, inverse_ref),
                (dtn_in, dtn_ref),
                (mass_in, mass_ref),
            ]
        )
    ]
    for load in loads:
        load.start()

    barrier = pltpu.get_barrier_semaphore()

    def greet(mode, mer):
        pl.semaphore_signal(barrier, inc=1, device_id=at(mode, mer), device_id_type=MESH)

    for k in range(1, n_mode):
        greet(other_mode(k), d)

    @pl.when(has_prev)
    def _():
        for k in range(n_mode):
            greet(other_mode(k), d - 1)

    @pl.when(has_next)
    def _():
        for k in range(n_mode):
            greet(other_mode(k), d + 1)

    for k in range(1, n_mer):
        peer = other_mer(k)

        @pl.when(jnp.logical_and(peer != d - 1, peer != d + 1))
        def _():
            greet(me, peer)

    s_f = 0
    s_eo = s_f + n_mode
    s_ep = s_eo + n_mode
    s_en = s_ep + n_mode
    s_fp = s_en + n_mode
    s_fn = s_fp + 1
    s_t = s_fn + 1
    s_c = s_t + n_mer

    def copy(src, dst, sec, out_no, in_no, mode, mer):
        return pltpu.make_async_remote_copy(
            src_ref=src,
            dst_ref=dst,
            send_sem=send_sem.at[sec, out_no],
            recv_sem=recv_sem.at[sec, in_no],
            device_id=at(mode, mer),
            device_id_type=MESH,
        )

    def f_copies(sec):
        return [
            copy(f_part.at[sec, other_mode(k)], f_got.at[sec, me], sec, s_f + other_mode(k), s_f + me, other_mode(k), d)
            for k in range(1, n_mode)
        ]

    def t_copies(sec):
        return [
            copy(t_part.at[sec], t_got.at[sec, d], sec, s_t + other_mer(k), s_t + d, me, other_mer(k))
            for k in range(1, n_mer)
        ]

    def up_copies(sec):
        made = [copy(f_full.at[sec], f_prev.at[sec], sec, s_fp, s_fp, me, d + 1)]
        if sec == 0:
            made.append(copy(connect_ref, c_prev, sec, s_c, s_c, me, d + 1))
        return made

    def down_copies(sec):
        return [copy(f_full.at[sec, :, pl.ds(0, GHOST)], f_next.at[sec], sec, s_fn, s_fn, me, d - 1)]

    def e_copies(sec):
        return [
            copy(e_part.at[sec, other_mode(k)], e_own.at[sec, me], sec, s_eo + other_mode(k), s_eo + me, other_mode(k), d)
            for k in range(1, n_mode)
        ]

    def e_up_copies(sec):
        return [
            copy(e_part.at[sec, other_mode(k)], e_prev.at[sec, me], sec, s_ep + other_mode(k), s_ep + me, other_mode(k), d + 1)
            for k in range(n_mode)
        ]

    def e_down_copies(sec):
        return [
            copy(e_part.at[sec, other_mode(k)], e_next.at[sec, me], sec, s_en + other_mode(k), s_en + me, other_mode(k), d - 1)
            for k in range(n_mode)
        ]

    sends_down = jnp.logical_and(has_prev, me < ghosts)

    def start(copies):
        for c in copies:
            c.start()

    def sent(copies):
        for c in copies:
            c.wait_send()

    def arrive(ref, sec, no):
        copy(ref, ref, sec, no, no, me, d).wait_recv()

    halves = 128 // wall_dev

    def stage(sec, value):
        low = value.astype(BF)
        f_full[sec] = low
        for j in range(n_mode):
            f_part[sec, j] = low[:, j * chunk : (j + 1) * chunk]
        f_got[sec, me] = f_part[sec, me]

    def stage_trace(sec):
        low = f_full[sec]
        picked = jnp.concatenate([low[r * mode_dev : (r + 1) * mode_dev] for r in (2, 5)], 0)
        walls = mm(picked, wall_hot[...]).astype(BF)
        t_part[sec] = walls
        t_got[sec, d] = walls

    def send_field(sec):
        start(f_copies(sec))

        @pl.when(has_next)
        def _():
            start(up_copies(sec))

        @pl.when(has_prev)
        def _():
            start(down_copies(sec))

    loads[0].wait()
    field = field_ref[...].reshape(rows, nodes)
    stage(0, field)

    @pl.when(jnp.logical_not(has_prev))
    def _():
        f_prev[...] = jnp.zeros(f_prev.shape, BF)
        e_prev[...] = jnp.zeros(e_prev.shape, BF)
        c_prev[...] = jnp.full(c_prev.shape, -1, jnp.int32)

    @pl.when(jnp.logical_not(has_next))
    def _():
        f_next[...] = jnp.zeros(f_next.shape, BF)
        e_next[...] = jnp.zeros(e_next.shape, BF)

    prev_n = has_prev.astype(jnp.int32)
    next_n = has_next.astype(jnp.int32)
    pl.semaphore_wait(barrier, n_mode - 1 + n_mer - 1 + (n_mode - 1) * (prev_n + next_n))

    loads[1].wait()
    send_field(0)

    step = 128

    def fill_pick(which, ref):
        numbers = jnp.concatenate([ref[e : e + 1, :] for e in range(elems)], 1)

        def fill(i, carry):
            base = pl.multiple_of(i * step, step)
            pick[which, pl.ds(base, step), :] = onehot(iota((step, slots), 0) + base == numbers)
            return carry

        lax.fori_loop(0, ext // step, fill, 0)

    loads[2].wait()
    wall_row = jnp.concatenate([wall_ref[...]] * halves, 1)
    lane = iota((1, 128), 1)
    wall_row = jnp.where(lane // wall_dev == lax.rem(d, halves), wall_row, -1)
    wall_hot[...] = onehot(iota((nodes, 128), 0) == wall_row)
    stage_trace(0)
    start(t_copies(0))

    fill_pick(0, connect_ref)

    wide_dim = 256
    group = wide_dim // npe
    groups = slots // wide_dim
    same = iota((wide_dim, wide_dim), 0) // npe == iota((wide_dim, wide_dim), 1) // npe

    def spread(ref, sign):
        turned = jnp.concatenate([sign * ref[...].T] * group, 1)
        return jnp.where(same, jnp.concatenate([turned] * group, 0), 0.0).astype(BF)

    loads[3].wait()
    kmat[0] = spread(stiff_ref, -1.0)
    loads[4].wait()
    kmat[1] = spread(curl_ref, 1.0)

    for load in loads[5:]:
        load.wait()
    mass_inv = 1.0 / mass_ref[...]
    mode_no = me * mode_dev + lax.rem(iota((rows, 1), 0), mode_dev)
    damp = 4.0 * (mode_no.astype(F32) / modes) ** 2

    def local(own, nxt, prv, which):
        here = mm(jnp.concatenate([own, nxt], 1), pick[0]).astype(BF)
        back = mm(jnp.concatenate([prv, own[:, :GHOST]], 1), pick[1]).astype(BF)
        tall = jnp.concatenate(
            [x[:, g * wide_dim : (g + 1) * wide_dim] for x in (here, back) for g in range(groups)], 0
        )
        done = mm(tall, kmat[which])
        return [done[i * rows : (i + 1) * rows] for i in range(2 * groups)]

    def scatter(parts):
        low = [x.astype(BF) for x in parts]
        total = mm_t(jnp.concatenate(low[:groups], 1), pick[0, :nodes, :])
        extra = mm_t(jnp.concatenate(low[groups:], 1), pick[1, nodes:, :])
        return jnp.concatenate([total[:, :GHOST] + extra, total[:, GHOST:]], 1)

    def lanes(ref, sec, count):
        return jnp.concatenate([ref[sec, j] for j in range(count)], 1)

    def rate(sec, value):
        for k in range(1, n_mode):
            arrive(f_got.at[sec, other_mode(k)], sec, s_f + other_mode(k))
        phys = mm(forward_ref[...].astype(BF), f_got[sec].reshape(n_mode * rows, chunk))
        px, py, pz = [phys[c * nphi : (c + 1) * nphi] for c in range(3)]
        vx, vy, vz = [vel_ref[c].astype(F32) for c in range(3)]
        cross = jnp.concatenate([vy * pz - vz * py, vz * px - vx * pz, vx * py - vy * px], 0)
        emf = mm(inverse_ref[...].astype(BF), cross.astype(BF)).astype(BF)
        e_part[sec] = emf.reshape(n_mode, rows, chunk)
        e_own[sec, me] = e_part[sec, me]
        start(e_copies(sec))

        @pl.when(has_next)
        def _():
            start(e_up_copies(sec))

        @pl.when(sends_down)
        def _():
            start(e_down_copies(sec))

        if sec == 0:

            @pl.when(has_prev)
            def _():
                arrive(c_prev, sec, s_c)

            fill_pick(1, c_prev)

        @pl.when(has_prev)
        def _():
            arrive(f_prev.at[sec], sec, s_fp)

        @pl.when(has_next)
        def _():
            arrive(f_next.at[sec], sec, s_fn)

        diffused = local(f_full[sec], f_next[sec], f_prev[sec], 0)

        for k in range(1, n_mer):
            arrive(t_got.at[sec, other_mer(k)], sec, s_t + other_mer(k))
        trace = jnp.concatenate(
            [sum([t_got[sec, i + h] for h in range(1, halves)], t_got[sec, i]) for i in range(0, n_mer, halves)], 1
        )
        wide = mm_t(trace, dtn_ref[...].reshape(mode_dev * wall_dev, trace.shape[1]))
        wide = jnp.where(iota(wide.shape, 1) // wall_dev == lax.rem(iota(wide.shape, 0), mode_dev), wide, 0.0)
        folded = sum([wide[:, i : i + 128] for i in range(128, wide.shape[1], 128)], wide[:, :128])
        flux = sum([folded[:, h * wall_dev : (h + 1) * wall_dev] for h in range(1, halves)], folded[:, :wall_dev])
        for m in range(mode_dev):
            flux_ref[sec, m] = jnp.concatenate([flux[m : m + 1], flux[mode_dev + m : mode_dev + m + 1]], 0)
        spots = mm_t(jnp.concatenate([-0.5 * flux] * halves, 1).astype(BF), wall_hot[...])
        blank = jnp.zeros((2 * mode_dev, nodes), F32)
        pulled = jnp.concatenate([blank, spots[:mode_dev], blank, spots[mode_dev:]], 0)

        for k in range(1, n_mode):
            arrive(e_own.at[sec, other_mode(k)], sec, s_eo + other_mode(k))

        @pl.when(has_prev)
        def _():
            for j in range(n_mode):
                arrive(e_prev.at[sec, j], sec, s_ep + j)

        @pl.when(has_next)
        def _():
            for j in range(ghosts):
                arrive(e_next.at[sec, j], sec, s_en + j)

        curled = local(lanes(e_own, sec, n_mode), lanes(e_next, sec, ghosts), lanes(e_prev, sec, n_mode), 1)
        total = scatter([x + y for x, y in zip(diffused, curled)]) + pulled
        return total * mass_inv - damp * value

    section = field + 0.2 * rate(0, field)
    stage(1, section)
    send_field(1)
    stage_trace(1)
    start(t_copies(1))
    second = rate(1, section)
    advanced = 0.5 * (field + section + 0.2 * second)
    out_ref[...] = advanced.reshape(out_ref.shape)

    for sec in range(2):
        sent(f_copies(sec))
        sent(t_copies(sec))
        sent(e_copies(sec))

        @pl.when(has_next)
        def _():
            sent(up_copies(sec))
            sent(e_up_copies(sec))

        @pl.when(has_prev)
        def _():
            sent(down_copies(sec))

        @pl.when(sends_down)
        def _():
            sent(e_down_copies(sec))


def finish(out_in, flux_in, out_ref, flux_ref, out_mid, flux_mid, sem):
    routes = [(flux_in, flux_mid, flux_ref), (out_in, out_mid, out_ref)]
    inward = [pltpu.make_async_copy(a, b, sem.at[i]) for i, (a, b, _) in enumerate(routes)]
    outward = [pltpu.make_async_copy(b, c, sem.at[2 + i]) for i, (_, b, c) in enumerate(routes)]
    for c in inward:
        c.start()
    for c, then in zip(inward, outward):
        c.wait()
        then.start()
    for c in outward:
        c.wait()


def body(field, velocity, stiffness, curl_matrix, mass, connect, wall_index, dtn):
    n_mode = lax.axis_size("mode")
    n_mer = lax.axis_size("mer")
    mode_dev, _, nodes = field.shape
    modes = mode_dev * n_mode
    nphi = velocity.shape[1]
    elems, npe = connect.shape
    wall_dev = wall_index.shape[0]
    rows = mode_dev * 6
    chunk = nodes // n_mode
    ghosts = GHOST // chunk
    forward, inverse = transforms(modes, mode_dev, nphi)
    sems = 4 * n_mode + n_mer + 3
    vmem = pl.BlockSpec(memory_space=pltpu.VMEM)
    hbm = pl.BlockSpec(memory_space=pltpu.HBM)
    shapes = (
        jax.ShapeDtypeStruct((6, mode_dev, nodes), F32),
        jax.ShapeDtypeStruct((2, mode_dev, 2, wall_dev), F32),
    )
    advanced, flux = pl.pallas_call(
        functools.partial(kernel, n_mode, n_mer, modes),
        out_shape=shapes,
        in_specs=[hbm] * 10,
        out_specs=(vmem, vmem),
        scratch_shapes=[
            pltpu.VMEM((2, rows, nodes), BF),
            pltpu.VMEM((2, n_mode, rows, chunk), BF),
            pltpu.VMEM((2, n_mode, rows, chunk), BF),
            pltpu.VMEM((2, rows, nodes), BF),
            pltpu.VMEM((2, rows, GHOST), BF),
            pltpu.VMEM((2, n_mode, rows, chunk), BF),
            pltpu.VMEM((2, n_mode, rows, chunk), BF),
            pltpu.VMEM((2, n_mode, rows, chunk), BF),
            pltpu.VMEM((2, ghosts, rows, chunk), BF),
            pltpu.VMEM((2, 2 * mode_dev, 128), BF),
            pltpu.VMEM((2, n_mer, 2 * mode_dev, 128), BF),
            pltpu.VMEM((elems, npe), jnp.int32),
            pltpu.VMEM((2, 256, 256), BF),
            pltpu.VMEM((2, nodes + GHOST, elems * npe), BF),
            pltpu.VMEM((nodes, 128), BF),
            pltpu.VMEM((6, mode_dev, nodes), F32),
            pltpu.VMEM(velocity.shape, BF),
            pltpu.VMEM(stiffness.shape, F32),
            pltpu.VMEM(curl_matrix.shape, F32),
            pltpu.VMEM((1, nodes), F32),
            pltpu.VMEM(connect.shape, jnp.int32),
            pltpu.VMEM((1, wall_dev), jnp.int32),
            pltpu.VMEM(dtn.shape, BF),
            pltpu.VMEM(forward.shape, F32),
            pltpu.VMEM(inverse.shape, F32),
            pltpu.SemaphoreType.DMA((2, sems)),
            pltpu.SemaphoreType.DMA((2, sems)),
            pltpu.SemaphoreType.DMA((10,)),
        ],
        compiler_params=pltpu.CompilerParams(
            collective_id=0, has_side_effects=True, vmem_limit_bytes=60 * 1024 * 1024
        ),
    )(
        jnp.swapaxes(field, 0, 1),
        velocity,
        stiffness,
        curl_matrix,
        mass.reshape(1, nodes),
        connect,
        wall_index.reshape(1, wall_dev),
        dtn,
        forward,
        inverse,
    )
    advanced, flux = pl.pallas_call(
        finish,
        out_shape=shapes,
        in_specs=[hbm] * 2,
        out_specs=(hbm, hbm),
        scratch_shapes=[
            pltpu.VMEM(shapes[0].shape, F32),
            pltpu.VMEM(shapes[1].shape, F32),
            pltpu.SemaphoreType.DMA((4,)),
        ],
        compiler_params=pltpu.CompilerParams(vmem_limit_bytes=60 * 1024 * 1024),
    )(advanced, flux)
    return jnp.swapaxes(advanced, 0, 1), flux


def solution(mesh):
    placed = (
        P("mode", None, "mer"),
        P(None, None, ("mer", "mode")),
        P(),
        P(),
        P("mer"),
        P("mer", None),
        P("mer"),
        P("mode", "mer", None),
    )
    return jax.shard_map(
        body,
        mesh=mesh,
        in_specs=placed,
        out_specs=(P("mode", None, "mer"), P(None, "mode", None, "mer")),
        check_vma=False,
    )
```
